32 devices in a mesh: subj: 2 (over x), ha: 8 (over z, y), dev: 2 (over core).
Axes of the slice: x: 2, y: 2, z: 4, core: 2. Of those that a mesh axis runs over, the one named last changes fastest.
Arguments:
- brain_image: float32 [64, 256, 768], P('subj', 'ha', 'dev'), parts along dimension 0, may hold values from -6 to 6
- adjoint_field: float32 [64, 256, 768], P('subj', 'ha', 'dev'), parts along dimension 0, may hold values from -6 to 6
- velocity_modes: float32 [6, 16, 32, 32], P('subj'), parts along dimension 0, may hold values from -4 to 4
Outputs:
- adjoint_end: float32 [64, 256, 768], P('subj', 'ha', 'dev'), parts along dimension 0
- image_end: float32 [64, 256, 768], P('subj', 'ha', 'dev'), parts along dimension 0
- velocity_next: float32 [6, 16, 32, 32], P('subj'), parts along dimension 0
The draws below stay inside these ranges and needn't reach their ends.
There are 2 independent parts, one for each index of `subj`. The reference program is written for one: setup_inputs(seed, part) draws one part's arguments, and reference() takes and returns one part's arrays. A program takes and returns all parts, laid end to end along the dimension named above; each array names one. Nothing has to cross between parts.
All inputs are finite; a program needn't handle non-finite values.
Results may differ from the reference program's by a relative error of at most 0.0003.
Values sent between devices are 32-bit elements; how exact they have to be, the bound alone decides.
No kernel may reach another device: no remote copies, remote signals or barrier semaphores. Data moves between devices by JAX's collectives and lax.ppermute only.
A program may use at most 128 MiB of HBM per device.

```python
import math
import jax
import jax.numpy as jnp
from jax import lax

PLANES = 32
MX = 16
M = 32
STEPS = 4
NY = 256
NZ = 768


def levels(key, extent, pieces, least, largest):
    loudness, own = 1.0, jax.random.fold_in(key, 6)
    for dim, shards_of in pieces:
        heights = jnp.exp(jax.random.uniform(jax.random.fold_in(own, dim), (shards_of,), jnp.float32, least / len(pieces), largest / len(pieces)))
        loudness = loudness * jnp.repeat(heights, extent[dim] // shards_of).reshape([-1 if axis == dim else 1 for axis in range(len(extent))])
    return loudness


def noise(stream_key, shape, deviation, reach, pieces=(), held_as=jnp.bfloat16):
    result = deviation * jax.random.normal(stream_key, shape, jnp.float32)
    if pieces:
        result = result * levels(stream_key, shape, pieces, -0.22, 0.18)
    return jnp.clip(result, -reach, reach).astype(held_as)


def setup_inputs(seed: int = 0, part: int = 0) -> dict:
    arg_keys = jax.random.split(jax.random.key(seed), 4)
    part_splits = jax.random.split(jax.random.fold_in(arg_keys[3], part), 4)
    return {
        "brain_image": noise(part_splits[0], (PLANES, NY, NZ), 1.0, 6.0, ((1, 8), (2, 2)), jnp.float32),
        "adjoint_field": noise(part_splits[1], (PLANES, NY, NZ), 1.0, 6.0, ((1, 8), (2, 2)), jnp.float32),
        "velocity_modes": noise(part_splits[2], (3, MX, M, M), 0.7, 4.0, (), jnp.float32),
    }


PRECISE = lax.Precision.HIGHEST
STEP_SIZE = 4.0
STIFFNESS = 2.0

def fourier_table(positions, length, modes):
    column = jnp.arange(modes, dtype=jnp.int32)
    middle_mode = modes // 2
    wavenumber = jnp.where(column <= middle_mode, column, column - middle_mode)
    phase_index = positions[:, None] * wavenumber[None, :] % length
    angles = phase_index.astype(jnp.float32) * (2.0 * math.pi / length)
    return jnp.where(column[None, :] <= middle_mode, jnp.cos(angles), jnp.sin(angles))

def dimension_terms(length, modes):
    column = jnp.arange(modes, dtype=jnp.int32)
    middle_mode = modes // 2
    wavenumber = jnp.where(column <= middle_mode, column, column - middle_mode)
    eigenvalue = 2.0 - 2.0 * jnp.cos(wavenumber.astype(jnp.float32) * (2.0 * math.pi / length))
    weight = jnp.where(column == 0, jnp.float32(length), jnp.float32(length / 2.0))
    return (eigenvalue, weight)

def mode_factor(planes, height, depth, modes_x, modes_yz):
    eigen_x, weight_x = dimension_terms(planes, modes_x)
    eigen_y, weight_y = dimension_terms(height, modes_yz)
    eigen_z, weight_z = dimension_terms(depth, modes_yz)
    eigenvalue = eigen_x[:, None, None] + eigen_y[None, :, None] + eigen_z[None, None, :]
    squared_norm = weight_x[:, None, None] * weight_y[None, :, None] * weight_z[None, None, :]
    mode_count = modes_x * modes_yz * modes_yz
    factor = STEP_SIZE * math.sqrt(mode_count) / (squared_norm * jnp.square(1.0 + STIFFNESS * eigenvalue))
    return factor.reshape(-1)

def expand(coeffs, table_x, table_y, table_z):
    mode_count = coeffs.shape[1] * coeffs.shape[2] * coeffs.shape[3]
    scaled = coeffs * (1.0 / math.sqrt(mode_count))
    inner = jnp.einsum('cabk,xa->cxbk', scaled, table_x, precision=PRECISE)
    inner = jnp.einsum('cxbk,yb->cxyk', inner, table_y, precision=PRECISE)
    return jnp.einsum('cxyk,zk->cxyz', inner, table_z, precision=PRECISE)

def project(forcing, table_x, table_y, table_z):
    inner = jnp.einsum('cxyz,zk->cxyk', forcing, table_z, precision=PRECISE)
    inner = jnp.einsum('cxyk,yb->cxbk', inner, table_y, precision=PRECISE)
    return jnp.einsum('cxbk,xa->cabk', inner, table_x, precision=PRECISE)

def upwind_rate(padded, speed):
    center = padded[1:-1, 1:-1, 1:-1]
    behind = (center - padded[:-2, 1:-1, 1:-1], center - padded[1:-1, :-2, 1:-1], center - padded[1:-1, 1:-1, :-2])
    ahead = (padded[2:, 1:-1, 1:-1] - center, padded[1:-1, 2:, 1:-1] - center, padded[1:-1, 1:-1, 2:] - center)
    summed = jnp.zeros_like(center)
    for direction in range(3):
        summed = summed + jnp.maximum(speed[direction], 0.0) * behind[direction] + jnp.minimum(speed[direction], 0.0) * ahead[direction]
    return -summed

def central_gradient(padded):
    return jnp.stack([0.5 * (padded[2:, 1:-1, 1:-1] - padded[:-2, 1:-1, 1:-1]), 0.5 * (padded[1:-1, 2:, 1:-1] - padded[1:-1, :-2, 1:-1]), 0.5 * (padded[1:-1, 1:-1, 2:] - padded[1:-1, 1:-1, :-2])])

def advance(current, speed):
    middle = current + 1.0 * upwind_rate(jnp.pad(current, 1), speed)
    second = upwind_rate(jnp.pad(middle, 1), speed)
    return 0.5 * (current + middle + 1.0 * second)

def reference(brain_image, adjoint_field, velocity_modes):
    planes, height, depth = brain_image.shape
    modes_x = velocity_modes.shape[1]
    modes_yz = velocity_modes.shape[2]
    table_x = fourier_table(jnp.arange(planes, dtype=jnp.int32), planes, modes_x)
    table_y = fourier_table(jnp.arange(height, dtype=jnp.int32), height, modes_yz)
    table_z = fourier_table(jnp.arange(depth, dtype=jnp.int32), depth, modes_yz)
    old_speed = expand(velocity_modes, table_x, table_y, table_z)
    backward = -old_speed
    current = adjoint_field
    for repeat in range(STEPS):
        current = advance(current, backward)
    adjoint_end = current
    forcing = adjoint_end[None] * central_gradient(jnp.pad(brain_image, 1))
    partial_value = project(forcing, table_x, table_y, table_z).reshape(3, -1)
    factor = mode_factor(planes, height, depth, modes_x, modes_yz)
    flat_next = velocity_modes.reshape(3, -1) + factor[None, :] * partial_value
    velocity_next = flat_next.reshape(velocity_modes.shape)
    new_speed = expand(velocity_next, table_x, table_y, table_z)
    current = brain_image
    for repeat in range(STEPS):
        current = advance(current, new_speed)
    return (adjoint_end, current, velocity_next)
```

```python
import math

import jax
import jax.numpy as jnp
from jax import lax
from jax.sharding import PartitionSpec as P

STEPS = 4


PRECISE = lax.Precision.HIGHEST
STEP_SIZE = 4.0
STIFFNESS = 2.0


def padded_2(cells, sides, width):
    for axis, dim in sides:
        count = lax.axis_size(axis)
        ends = count - 1
        head = lax.slice_in_dim(cells, 0, width, axis=dim)
        tail = lax.slice_in_dim(cells, cells.shape[dim] - width, cells.shape[dim], axis=dim)
        cells = jnp.concatenate(
            [
                lax.ppermute(tail, axis, [(i, (i + 1) % count) for i in range(ends)]),
                cells,
                lax.ppermute(head, axis, [((i + 1) % count, i) for i in range(ends)]),
            ],
            axis=dim,
        )
    return cells


def fourier_table(positions, length, modes):
    column = jnp.arange(modes, dtype=jnp.int32)
    middle_mode = modes // 2
    wavenumber = jnp.where(column <= middle_mode, column, column - middle_mode)
    phase_index = positions[:, None] * wavenumber[None, :] % length
    angles = phase_index.astype(jnp.float32) * (2.0 * math.pi / length)
    return jnp.where(column[None, :] <= middle_mode, jnp.cos(angles), jnp.sin(angles))


def dimension_terms(length, modes):
    column = jnp.arange(modes, dtype=jnp.int32)
    middle_mode = modes // 2
    wavenumber = jnp.where(column <= middle_mode, column, column - middle_mode)
    eigenvalue = 2.0 - 2.0 * jnp.cos(wavenumber.astype(jnp.float32) * (2.0 * math.pi / length))
    weight = jnp.where(column == 0, jnp.float32(length), jnp.float32(length / 2.0))
    return (eigenvalue, weight)


def mode_factor(planes, height, depth, modes_x, modes_yz):
    eigen_x, weight_x = dimension_terms(planes, modes_x)
    eigen_y, weight_y = dimension_terms(height, modes_yz)
    eigen_z, weight_z = dimension_terms(depth, modes_yz)
    eigenvalue = eigen_x[:, None, None] + eigen_y[None, :, None] + eigen_z[None, None, :]
    squared_norm = weight_x[:, None, None] * weight_y[None, :, None] * weight_z[None, None, :]
    mode_count = modes_x * modes_yz * modes_yz
    factor = (
        STEP_SIZE
        * math.sqrt(mode_count)
        / (squared_norm * jnp.square(1.0 + STIFFNESS * eigenvalue))
    )
    return factor.reshape(-1)


def expand(coeffs, table_x, table_y, table_z):
    mode_count = coeffs.shape[1] * coeffs.shape[2] * coeffs.shape[3]
    scaled = coeffs * (1.0 / math.sqrt(mode_count))
    inner = jnp.einsum("cabk,xa->cxbk", scaled, table_x, precision=PRECISE)
    inner = jnp.einsum("cxbk,yb->cxyk", inner, table_y, precision=PRECISE)
    return jnp.einsum("cxyk,zk->cxyz", inner, table_z, precision=PRECISE)


def project(forcing, table_x, table_y, table_z):
    inner = jnp.einsum("cxyz,zk->cxyk", forcing, table_z, precision=PRECISE)
    inner = jnp.einsum("cxyk,yb->cxbk", inner, table_y, precision=PRECISE)
    return jnp.einsum("cxbk,xa->cabk", inner, table_x, precision=PRECISE)


def upwind_rate(padded, speed):
    center = padded[1:-1, 1:-1, 1:-1]
    behind = (
        center - padded[:-2, 1:-1, 1:-1],
        center - padded[1:-1, :-2, 1:-1],
        center - padded[1:-1, 1:-1, :-2],
    )
    ahead = (
        padded[2:, 1:-1, 1:-1] - center,
        padded[1:-1, 2:, 1:-1] - center,
        padded[1:-1, 1:-1, 2:] - center,
    )
    summed = jnp.zeros_like(center)
    for direction in range(3):
        summed = (
            summed
            + jnp.maximum(speed[direction], 0.0) * behind[direction]
            + jnp.minimum(speed[direction], 0.0) * ahead[direction]
        )
    return -summed


def central_gradient(padded):
    return jnp.stack(
        [
            0.5 * (padded[2:, 1:-1, 1:-1] - padded[:-2, 1:-1, 1:-1]),
            0.5 * (padded[1:-1, 2:, 1:-1] - padded[1:-1, :-2, 1:-1]),
            0.5 * (padded[1:-1, 1:-1, 2:] - padded[1:-1, 1:-1, :-2]),
        ]
    )


def pad_planes(field):
    return jnp.pad(field, ((1, 1), (0, 0), (0, 0)))


def rim_cells(field):
    return padded_2(field, (("ha", 1), ("dev", 2)), 1)


def advance_pair(current, speed, inside):
    widened = pad_planes(padded_2(current, (("ha", 1), ("dev", 2)), 4))
    start = widened[1:-1, 1:-1, 1:-1]
    middle = (start + 1.0 * upwind_rate(widened, speed)) * inside
    second = upwind_rate(pad_planes(middle), speed[:, :, 1:-1, 1:-1])
    stepped = (
        0.5 * (start[:, 1:-1, 1:-1] + middle[:, 1:-1, 1:-1] + 1.0 * second) * inside[1:-1, 1:-1]
    )
    middle_two = (
        stepped[:, 1:-1, 1:-1] + 1.0 * upwind_rate(pad_planes(stepped), speed[:, :, 2:-2, 2:-2])
    ) * inside[2:-2, 2:-2]
    second_two = upwind_rate(pad_planes(middle_two), speed[:, :, 3:-3, 3:-3])
    return 0.5 * (stepped[:, 2:-2, 2:-2] + middle_two[:, 1:-1, 1:-1] + 1.0 * second_two)


def transport(start_field, speed, inside):
    current = start_field
    for repeat in range(STEPS // 2):
        current = advance_pair(current, speed, inside)
    return current


def swap_with(value, axis, step):
    count = lax.axis_size(axis)
    return lax.ppermute(value, axis, [(i, i ^ step) for i in range(count)])


def sum_over_pair_steps(value):
    count_height = lax.axis_size("ha")
    packed = value.reshape(2, -1, 128)
    side = lax.axis_index("dev")
    kept = lax.dynamic_index_in_dim(packed, side, 0, False)
    given = lax.dynamic_index_in_dim(packed, 1 - side, 0, False)
    kept = kept + swap_with(given, "dev", 1)
    step = 1
    while step < count_height:
        kept = kept + swap_with(kept, "ha", step)
        step *= 2
    other = swap_with(kept, "dev", 1)
    first = jnp.where(side == 0, kept, other)
    second = jnp.where(side == 0, other, kept)
    return jnp.stack([first, second]).reshape(value.shape)


def per_device(brain_image, adjoint_field, velocity_modes):
    planes, rows_height, rows_depth = brain_image.shape
    count_height = lax.axis_size("ha")
    count_depth = lax.axis_size("dev")
    height = rows_height * count_height
    depth = rows_depth * count_depth
    modes_x = velocity_modes.shape[1]
    modes_yz = velocity_modes.shape[2]
    index_height = lax.axis_index("ha")
    index_depth = lax.axis_index("dev")
    margin = 3
    rows_y = (
        index_height * rows_height - margin + jnp.arange(rows_height + 2 * margin, dtype=jnp.int32)
    )
    rows_z = (
        index_depth * rows_depth - margin + jnp.arange(rows_depth + 2 * margin, dtype=jnp.int32)
    )
    inside = (
        ((rows_y >= 0) & (rows_y < height))[:, None] & ((rows_z >= 0) & (rows_z < depth))[None, :]
    ).astype(jnp.float32)
    table_x = fourier_table(jnp.arange(planes, dtype=jnp.int32), planes, modes_x)
    table_y = fourier_table(rows_y, height, modes_yz)
    table_z = fourier_table(rows_z, depth, modes_yz)
    core_y = table_y[margin : margin + rows_height]
    core_z = table_z[margin : margin + rows_depth]
    old_speed = expand(velocity_modes, table_x, table_y, table_z)
    backward = -old_speed
    adjoint_end = transport(adjoint_field, backward, inside)
    forcing = adjoint_end[None] * central_gradient(pad_planes(rim_cells(brain_image)))
    partial_value = project(forcing, table_x, core_y, core_z).reshape(3, -1)
    factor = mode_factor(planes, height, depth, modes_x, modes_yz)
    flat_old = velocity_modes.reshape(3, -1)
    summed = sum_over_pair_steps(partial_value)
    updated = flat_old + factor[None, :] * summed
    velocity_next = updated.reshape(velocity_modes.shape)
    new_speed = expand(velocity_next, table_x, table_y, table_z)
    image_end = transport(brain_image, new_speed, inside)
    return (adjoint_end, image_end, velocity_next)


def solution(mesh):
    placed = (P("subj", "ha", "dev"), P("subj", "ha", "dev"), P("subj", None, None, None))
    return jax.shard_map(
        per_device,
        mesh=mesh,
        in_specs=placed,
        out_specs=(P("subj", "ha", "dev"), P("subj", "ha", "dev"), P("subj", None, None, None)),
        check_vma=False,
    )
```

```python
import functools
import math

import jax
import jax.numpy as jnp
import ml_dtypes
import numpy as np
from jax import lax
from jax.experimental import pallas as pl
from jax.experimental.pallas import tpu as pltpu
from jax.sharding import PartitionSpec as P

STEPS = 4
STEP_SIZE = 4.0
STIFFNESS = 2.0
HALO = 2 * STEPS
LANES = 128
SUB = 8
F32 = jnp.float32
BF16 = jnp.bfloat16
VMEM_LIMIT = 60 * 2**20


def wavenumbers(modes):
    column = np.arange(modes)
    return np.where(column <= modes // 2, column, column - modes // 2)


def fourier_table(positions, length, modes):
    column = np.arange(modes)
    angles = (positions[:, None] * wavenumbers(modes)[None, :] % length) * (2.0 * math.pi / length)
    table = np.where(column[None, :] <= modes // 2, np.cos(angles), np.sin(angles))
    inside = (positions >= 0) & (positions < length)
    return np.where(inside[:, None], table, 0.0)


def mode_factor(planes, height, depth, modes_x, modes_yz):
    def terms(length, modes):
        eigen = 2.0 - 2.0 * np.cos(wavenumbers(modes) * (2.0 * math.pi / length))
        return eigen, np.where(np.arange(modes) == 0, length, length / 2.0)

    ex, wx = terms(planes, modes_x)
    ey, wy = terms(height, modes_yz)
    ez, wz = terms(depth, modes_yz)
    eigen = ex[:, None, None] + ey[None, :, None] + ez[None, None, :]
    norm = wx[:, None, None] * wy[None, :, None] * wz[None, None, :]
    count = modes_x * modes_yz * modes_yz
    return STEP_SIZE * math.sqrt(count) / (norm * np.square(1.0 + STIFFNESS * eigen))


def split_np(table):
    high = table.astype(np.float32).astype(ml_dtypes.bfloat16)
    low = (table - high.astype(np.float64)).astype(ml_dtypes.bfloat16)
    return high, low


class Sizes:
    def __init__(self, planes, rows, depth, modes_x, modes, count_height, count_depth):
        self.planes, self.rows, self.depth = planes, rows, depth
        self.modes_x, self.modes = modes_x, modes
        self.count_height, self.count_depth = count_height, count_depth
        self.tall = rows + 2 * HALO
        self.phases = -(-(depth + 2 * HALO) // LANES)
        self.wide = self.phases * LANES
        self.groups = planes // SUB
        self.tiles = depth // LANES
        self.packs = LANES // modes
        self.pairs = modes_x * modes
        self.chunk = self.pairs // self.packs
        assert planes % SUB == 0 and depth % LANES == 0 and rows % HALO == 0
        assert self.packs == 4 and self.wide >= depth + 2 * HALO

    def tables(self):
        n = self
        order_x = np.array([n.groups * s + g for g in range(n.groups) for s in range(SUB)])
        order_z = np.array([n.phases * l + s for s in range(n.phases) for l in range(LANES)])
        table_x = fourier_table(order_x, n.planes, n.modes_x)
        height, depth = n.rows * n.count_height, n.depth * n.count_depth
        bx = np.repeat(table_x, n.modes, axis=1) / math.sqrt(n.pairs * n.modes)
        by, by_t, bz_e, bz_p = [], [], [], []
        for i in range(n.count_height):
            table_y = fourier_table(np.arange(n.tall) - HALO + i * n.rows, height, n.modes)
            by.append(np.tile(table_y, (1, n.modes_x)))
            own = table_y[HALO : HALO + n.rows]
            by_t.append(np.repeat(own.T, n.planes, axis=1))
        bx_t = np.tile(table_x.T, (1, n.rows))
        for i in range(n.count_depth):
            place = order_z - HALO
            reach = (place >= -HALO) & (place < n.depth + HALO)
            table_z = fourier_table(place + i * n.depth, depth, n.modes) * reach[:, None]
            high, low = split_np(table_z.T)
            bz_e.append(np.concatenate([high, high, low, np.zeros_like(low)]))
            own = ((place >= 0) & (place < n.depth))[:, None]
            high, low = split_np(0.5 * table_z * own)
            held = np.zeros((3, n.wide, 2 * LANES), ml_dtypes.bfloat16)
            for c in range(3):
                held[c, :, n.modes * c : n.modes * (c + 1)] = high
                held[c, :, LANES + n.modes * c : LANES + n.modes * (c + 1)] = low
            bz_p.append(held)
        spread = np.zeros((n.depth + LANES, n.wide), ml_dtypes.bfloat16)
        for column, position in enumerate(order_z):
            z = position - HALO
            if 0 <= z < n.depth:
                spread[z, column] = 1
            elif -HALO <= z < 0:
                spread[n.depth + LANES + z, column] = 1
            elif n.depth <= z < n.depth + HALO:
                spread[z, column] = 1
        gather = np.ascontiguousarray(spread[: n.depth].T)
        factor = mode_factor(n.planes, height, depth, n.modes_x, n.modes)
        factor = factor.reshape(n.packs, n.chunk, n.modes).transpose(1, 0, 2).reshape(n.chunk, LANES)
        return dict(
            bx=bx.astype(np.float32),
            by=np.stack(by).astype(np.float32),
            bx_t=bx_t.astype(np.float32),
            by_t=np.stack(by_t).astype(np.float32),
            bz_e=np.stack(bz_e),
            bz_p=np.stack(bz_p),
            spread=spread,
            gather=gather,
            factor=factor.astype(np.float32),
        )


def split(value):
    high = value.astype(BF16)
    return high, (value - high.astype(F32)).astype(BF16)


def dot(a, b):
    return jnp.dot(a, b, preferred_element_type=F32)


def unpacked(packed, c, n):
    lane = lax.broadcasted_iota(jnp.int32, (n.chunk, LANES), 1) // n.modes
    piece = packed[c * n.chunk : (c + 1) * n.chunk]
    parts = []
    for g in range(n.packs):
        held = jnp.where(lane == g, piece, 0.0)
        held = held + pltpu.roll(held, n.modes, 1)
        parts.append(held + pltpu.roll(held, 2 * n.modes, 1))
    return jnp.concatenate(parts, axis=0)


def expand_into(n, coeffs, w_ref, bx_ref, by_ref, bz_ref, speed):
    for c in range(3):
        high, low = split(coeffs[c])
        w_ref[:, c * LANES : (c + 1) * LANES] = high
        w_ref[:, (3 + c) * LANES : (4 + c) * LANES] = low
    chunk = SUB
    lane = lax.broadcasted_iota(jnp.int32, (chunk * n.planes, LANES), 1) // n.modes

    def body(i, _):
        rows = pl.ds(pl.multiple_of(i * chunk, chunk), chunk)
        by = by_ref[rows, :]
        bx = bx_ref[...]
        table = jnp.concatenate([bx * by[j : j + 1, :] for j in range(chunk)], axis=0)
        high, low = split(table)
        main = dot(high, w_ref[...])
        rest = dot(low, w_ref[:, : 3 * LANES])
        size = None
        for c in range(3):
            inner = (
                main[:, c * LANES : (c + 1) * LANES]
                + main[:, (3 + c) * LANES : (4 + c) * LANES]
                + rest[:, c * LANES : (c + 1) * LANES]
            )
            head = inner.astype(BF16).astype(F32)
            mixed = jnp.where(lane == 1, inner - head, head).astype(BF16)
            full = dot(mixed, bz_ref[...])
            size = jnp.abs(full) if c == 0 else size + jnp.abs(full)
            for s in range(n.phases):
                part = full[:, s * LANES : (s + 1) * LANES]
                speed[c, rows, s] = part.reshape(chunk, n.groups, SUB, LANES)
        for s in range(n.phases):
            part = 1.0 - size[:, s * LANES : (s + 1) * LANES]
            speed[3, rows, s] = part.reshape(chunk, n.groups, SUB, LANES)
        return 0

    lax.fori_loop(0, n.tall // chunk, body, 0)


def field_copies(n, own, low, high, side, side_low, side_high, raw, sems):
    count = n.planes * n.rows
    thin = n.planes * HALO
    jobs = []
    for t in range(n.tiles):
        cut = slice(t * LANES, (t + 1) * LANES)
        jobs.append((own.at[:, cut], raw.at[t, 0:count]))
        jobs.append((low.at[:, cut], raw.at[t, count : count + thin]))
        jobs.append((high.at[:, cut], raw.at[t, count + thin : count + 2 * thin]))
    jobs.append((side, raw.at[n.tiles, 0:count]))
    jobs.append((side_low, raw.at[n.tiles, count : count + thin]))
    jobs.append((side_high, raw.at[n.tiles, count + thin : count + 2 * thin]))
    return [pltpu.make_async_copy(a, b, sems.at[i]) for i, (a, b) in enumerate(jobs)]


def interleave(n, raw, spread, field):
    count = n.planes * n.rows
    thin = n.planes * HALO

    def chunk(first, base, rows, y_of, target):
        columns = []
        for t in range(n.tiles + 1):
            blocks = []
            for j in range(HALO):
                for g in range(n.groups):
                    start = base + g * rows + y_of + j
                    blocks.append(raw[t, pl.ds(start, SUB, stride=n.groups * rows), :])
            columns.append(jnp.concatenate(blocks, axis=0))
        value = jnp.concatenate(columns, axis=1)
        high, low = split(value)
        out = dot(high, spread[...]) + dot(low, spread[...])
        for s in range(n.phases):
            part = out[:, s * LANES : (s + 1) * LANES]
            field[target, s] = part.reshape(HALO, n.groups, SUB, LANES)

    chunk(0, count, HALO, 0, slice(0, HALO))
    chunk(0, count + thin, HALO, 0, slice(HALO + n.rows, 2 * HALO + n.rows))

    def body(i, _):
        y = pl.multiple_of(i * HALO, HALO)
        chunk(0, 0, n.rows, y, pl.ds(y + HALO, HALO))
        return 0

    lax.fori_loop(0, n.rows // HALO, body, 0)


def neighbours(n, field, y0, rows):
    held = {}
    sub = lax.broadcasted_iota(jnp.int32, (SUB, LANES), 0)
    first, last = sub == 0, sub == SUB - 1
    phases, groups = n.phases, n.groups

    def at(j, s, g):
        if (j, s, g) not in held:
            held[j, s, g] = field[y0 + j, s, g]
        return held[j, s, g]

    edges = {}
    for j in range(rows):
        for g in range(groups):
            edges["zp", j, g] = pltpu.roll(at(j, 0, g), LANES - 1, 1)
            edges["zm", j, g] = pltpu.roll(at(j, phases - 1, g), 1, 1)
        for s in range(phases):
            edges["xp", j, s] = jnp.where(last, 0.0, pltpu.roll(at(j, s, 0), SUB - 1, 0))
            edges["xm", j, s] = jnp.where(first, 0.0, pltpu.roll(at(j, s, groups - 1), 1, 0))

    def around(j, s, g):
        xm = at(j, s, g - 1) if g else edges["xm", j, s]
        xp = at(j, s, g + 1) if g < groups - 1 else edges["xp", j, s]
        zm = at(j, s - 1, g) if s else edges["zm", j, g]
        zp = at(j, s + 1, g) if s < phases - 1 else edges["zp", j, g]
        return at(j, s, g), (xm, at(j - 1, s, g), zm), (xp, at(j + 1, s, g), zp)

    return around


def upwind_rows(n, source, target, speed, y0, rows, second):
    around = neighbours(n, source, y0, rows)
    for j in range(rows):
        for s in range(n.phases):
            for g in range(n.groups):
                here, behind, ahead = around(j, s, g)
                total = speed[3, y0 + j, s, g] * here
                for d in range(3):
                    u = speed[d, y0 + j, s, g]
                    total = total + jnp.abs(u) * jnp.where(u > 0, behind[d], ahead[d])
                if second:
                    total = 0.5 * (target[y0 + j, s, g] + total)
                target[y0 + j, s, g] = total


def sweep(n, source, target, speed, low, high, second):
    count = (high - low) // 4
    lax.fori_loop(
        0,
        count,
        lambda i, _: (upwind_rows(n, source, target, speed, low + 4 * i, 4, second), 0)[1],
        0,
    )
    return low + 4 * count


def transport(n, field, spare, speed):
    tall = n.tall

    def step(r, _):
        first = 2 * r + 1
        done = sweep(n, field, spare, speed, first, tall - first, False)
        if (tall - 2) % 4:
            upwind_rows(n, field, spare, speed, done, 2, False)
        done = sweep(n, spare, field, speed, first + 1, tall - first - 1, True)
        if tall % 4:
            upwind_rows(n, spare, field, speed, done, 2, True)
        return 0

    lax.fori_loop(0, STEPS, step, 0)


def deinterleave(n, field, gather, out):
    def body(i, _):
        y = pl.multiple_of(i * HALO, HALO)
        columns = [
            field[pl.ds(y + HALO, HALO), s].reshape(HALO * n.planes, LANES) for s in range(n.phases)
        ]
        high, low = split(jnp.concatenate(columns, axis=1))
        value = dot(high, gather[...]) + dot(low, gather[...])
        for t in range(n.tiles):
            for j in range(HALO):
                for g in range(n.groups):
                    row = j * n.planes + g * SUB
                    out[t, pl.ds(g * n.rows + y + j, SUB, stride=n.groups * n.rows), :] = value[
                        row : row + SUB, t * LANES : (t + 1) * LANES
                    ]
        return 0

    lax.fori_loop(0, n.rows // HALO, body, 0)


def result_copies(n, out, target, sems):
    return [
        pltpu.make_async_copy(out.at[t], target.at[:, t * LANES : (t + 1) * LANES], sems.at[t])
        for t in range(n.tiles)
    ]


def force(n, adjoint, image, f_high, f_low):
    def body(y, _):
        around = neighbours(n, image, y + HALO, 1)
        for s in range(n.phases):
            pieces = [[], [], []]
            for g in range(n.groups):
                _, behind, ahead = around(0, s, g)
                end = adjoint[y + HALO, s, g]
                for d in range(3):
                    pieces[d].append(end * (ahead[d] - behind[d]))
            for d in range(3):
                high, low = split(jnp.concatenate(pieces[d], axis=0))
                rows = pl.ds(pl.multiple_of(y * n.planes, n.planes), n.planes)
                f_high[d, rows, s * LANES : (s + 1) * LANES] = high
                f_low[d, rows, s * LANES : (s + 1) * LANES] = low
        return 0

    lax.fori_loop(0, n.rows, body, 0)


def project(n, f_high, f_low, bz_ref, bx_ref, by_ref, total, packed):
    size = HALO * n.planes
    total[...] = jnp.zeros_like(total)

    def body(i, _):
        start = pl.multiple_of(i * size, size)
        rows = pl.ds(start, size)
        main, rest = None, None
        for d in range(3):
            one = dot(f_high[d, rows, :], bz_ref[d])
            two = dot(f_low[d, rows, :], bz_ref[d, :, :LANES])
            main = one if d == 0 else main + one
            rest = two if d == 0 else rest + two
        inner = main[:, :LANES] + main[:, LANES:] + rest
        high, low = split(inner)
        by = by_ref[:, rows]
        bx = bx_ref[:, rows]
        table = jnp.concatenate([by * bx[a : a + 1, :] for a in range(n.modes_x)], axis=0)
        t_high, t_low = split(table)
        both = dot(t_high, jnp.concatenate([high, low], axis=1))
        total[...] += both[:, :LANES] + both[:, LANES:] + dot(t_low, high)
        return 0

    lax.fori_loop(0, n.rows // HALO, body, 0)
    lane = lax.broadcasted_iota(jnp.int32, (n.chunk, LANES), 1) // n.modes
    for c in range(3):
        value = jnp.zeros((n.chunk, LANES), F32)
        for g in range(n.packs):
            piece = total[g * n.chunk : (g + 1) * n.chunk, :]
            shift = (n.modes * (g - c)) % LANES
            value = jnp.where(lane == g, pltpu.roll(piece, shift, 1) if shift else piece, value)
        packed[c * n.chunk : (c + 1) * n.chunk, :] = value


def first_kernel(n, _, modes, bx, by, bz_e, bz_p, bx_t, by_t, spread, gather, *rest):
    fields, rest = rest[:12], rest[12:]
    packed, end, speed, field, spare, image, raw_a, raw_b, w, f_high, f_low, total, sems = rest
    pulls_a = field_copies(n, *fields[:6], raw_a, sems.at[0])
    pulls_b = field_copies(n, *fields[6:], raw_b, sems.at[1])
    for copy in pulls_a + pulls_b:
        copy.start()
    coeffs = [-unpacked(modes[...], c, n) for c in range(3)]
    expand_into(n, coeffs, w, bx, by.at[0], bz_e.at[0], speed)
    for copy in pulls_a:
        copy.wait()
    interleave(n, raw_a, spread, field)
    transport(n, field, spare, speed)
    for copy in pulls_b:
        copy.wait()
    interleave(n, raw_b, spread, image)
    deinterleave(n, field, gather, raw_a.at[:, : n.planes * n.rows])
    pushes = result_copies(n, raw_a.at[:, : n.planes * n.rows], end, sems.at[2])
    for copy in pushes:
        copy.start()
    force(n, field, image, f_high, f_low)
    project(n, f_high, f_low, bz_p.at[0], bx_t, by_t.at[0], total, packed)
    for copy in pushes:
        copy.wait()


def second_kernel(n, _, modes, summed, factor, bx, by, bz_e, spread, gather, *rest):
    fields, rest = rest[:6], rest[6:]
    end, updated, speed, field, spare, raw, w, sems = rest
    pulls = field_copies(n, *fields, raw, sems.at[0])
    for copy in pulls:
        copy.start()
    scale = jnp.concatenate([factor[...]] * 3, axis=0)
    packed = modes[...] + scale * summed[...]
    coeffs = [unpacked(packed, c, n) for c in range(3)]
    for c in range(3):
        updated[c] = coeffs[c][:, : n.modes]
    expand_into(n, coeffs, w, bx, by.at[0], bz_e.at[0], speed)
    for copy in pulls:
        copy.wait()
    interleave(n, raw, spread, field)
    transport(n, field, spare, speed)
    deinterleave(n, field, gather, raw.at[:, : n.planes * n.rows])
    pushes = result_copies(n, raw.at[:, : n.planes * n.rows], end, sems.at[1])
    for copy in pushes:
        copy.start()
    for copy in pushes:
        copy.wait()


def swap_with(value, axis, step):
    count = lax.axis_size(axis)
    return lax.ppermute(value, axis, [(i, i ^ step) for i in range(count)])


def sum_over_devices(packed):
    count_height, count_depth = lax.axis_size("ha"), lax.axis_size("dev")
    if count_depth != 2 or count_height & (count_height - 1):
        return lax.psum(packed, ("ha", "dev"))
    halves = packed.reshape(2, -1, LANES)
    side = lax.axis_index("dev")
    kept = lax.dynamic_index_in_dim(halves, side, 0, False)
    given = lax.dynamic_index_in_dim(halves, 1 - side, 0, False)
    kept = kept + swap_with(given, "dev", 1)
    step = 1
    while step < count_height:
        kept = kept + swap_with(kept, "ha", step)
        step *= 2
    other = swap_with(kept, "dev", 1)
    first = jnp.where(side == 0, kept, other)
    second = jnp.where(side == 0, other, kept)
    return jnp.concatenate([first, second], axis=0)


def beside(cells):
    count = lax.axis_size("dev")
    index = lax.axis_index("dev")
    lane = lax.broadcasted_iota(jnp.int32, (1, 1, LANES), 2)
    head = jnp.where(lane < LANES // 2, cells[:, :, :LANES], 0.0)
    tail = jnp.where(lane >= LANES // 2, cells[:, :, -LANES:], 0.0)
    if count == 1:
        return jnp.zeros_like(head)
    if count == 2:
        return swap_with(jnp.where(index == 0, tail, head), "dev", 1)
    ends = range(count - 1)
    return lax.ppermute(tail, "dev", [(i, i + 1) for i in ends]) + lax.ppermute(
        head, "dev", [(i + 1, i) for i in ends]
    )


def with_halos(cells):
    ends = range(lax.axis_size("ha") - 1)
    low = lax.ppermute(cells[:, -HALO:], "ha", [(i, i + 1) for i in ends])
    high = lax.ppermute(cells[:, :HALO], "ha", [(i + 1, i) for i in ends])
    side = beside(cells)
    both = beside(jnp.concatenate([low, high], axis=1))
    parts = (cells, low, high, side, both[:, :HALO], both[:, HALO:])
    return [part.reshape(-1, part.shape[-1]) for part in parts]


def per_device(brain_image, adjoint_field, velocity_modes):
    planes, rows, depth = brain_image.shape
    n = Sizes(
        planes,
        rows,
        depth,
        velocity_modes.shape[1],
        velocity_modes.shape[2],
        lax.axis_size("ha"),
        lax.axis_size("dev"),
    )
    t = {name: jnp.asarray(value) for name, value in n.tables().items()}
    place = jnp.stack([lax.axis_index("ha"), lax.axis_index("dev")]).astype(jnp.int32)
    modes = velocity_modes.reshape(3, n.packs, n.chunk, n.modes).transpose(0, 2, 1, 3)
    modes = modes.reshape(3 * n.chunk, LANES)
    adjoint = with_halos(adjoint_field)
    image = with_halos(brain_image)

    whole = pl.BlockSpec(memory_space=pltpu.VMEM)
    outside = pl.BlockSpec(memory_space=pl.ANY)

    def picked(table, axis):
        zeros = (0,) * (table.ndim - 1)
        return pl.BlockSpec((1,) + table.shape[1:], lambda i, at: (at[axis],) + zeros)

    block = (n.tall, n.phases, n.groups, SUB, LANES)
    raw = pltpu.VMEM((n.tiles + 1, planes * n.tall, LANES), F32)
    pulls = 3 * n.tiles + 3
    packed_shape = (3 * n.chunk, LANES)
    flat = (planes * rows, depth)
    params = pltpu.CompilerParams(vmem_limit_bytes=VMEM_LIMIT)
    packed, adjoint_end = pl.pallas_call(
        functools.partial(first_kernel, n),
        grid_spec=pltpu.PrefetchScalarGridSpec(
            num_scalar_prefetch=1,
            grid=(1,),
            in_specs=[
                whole, whole, picked(t["by"], 0), picked(t["bz_e"], 1), picked(t["bz_p"], 1),
                whole, picked(t["by_t"], 0), whole, whole,
            ] + [outside] * 12,
            out_specs=[whole, outside],
            scratch_shapes=[
                pltpu.VMEM((4,) + block, F32),
                pltpu.VMEM(block, F32),
                pltpu.VMEM(block, F32),
                pltpu.VMEM(block, F32),
                raw,
                raw,
                pltpu.VMEM((n.pairs, 6 * LANES), BF16),
                pltpu.VMEM((3, planes * rows, n.wide), BF16),
                pltpu.VMEM((3, planes * rows, n.wide), BF16),
                pltpu.VMEM((n.pairs, LANES), F32),
                pltpu.SemaphoreType.DMA((3, pulls)),
            ],
        ),
        out_shape=[jax.ShapeDtypeStruct(packed_shape, F32), jax.ShapeDtypeStruct(flat, F32)],
        compiler_params=params,
    )(
        place, modes, t["bx"], t["by"], t["bz_e"], t["bz_p"], t["bx_t"], t["by_t"], t["spread"],
        t["gather"], *adjoint, *image,
    )
    summed = sum_over_devices(packed)
    image_end, updated = pl.pallas_call(
        functools.partial(second_kernel, n),
        grid_spec=pltpu.PrefetchScalarGridSpec(
            num_scalar_prefetch=1,
            grid=(1,),
            in_specs=[
                whole, whole, whole, whole, picked(t["by"], 0), picked(t["bz_e"], 1), whole, whole,
            ] + [outside] * 6,
            out_specs=[outside, whole],
            scratch_shapes=[
                pltpu.VMEM((4,) + block, F32),
                pltpu.VMEM(block, F32),
                pltpu.VMEM(block, F32),
                raw,
                pltpu.VMEM((n.pairs, 6 * LANES), BF16),
                pltpu.SemaphoreType.DMA((2, pulls)),
            ],
        ),
        out_shape=[
            jax.ShapeDtypeStruct(flat, F32),
            jax.ShapeDtypeStruct((3, n.pairs, n.modes), F32),
        ],
        compiler_params=params,
    )(place, modes, summed, t["factor"], t["bx"], t["by"], t["bz_e"], t["spread"], t["gather"], *image)
    return (
        adjoint_end.reshape(brain_image.shape),
        image_end.reshape(brain_image.shape),
        updated.reshape(velocity_modes.shape),
    )


def solution(mesh):
    placed = (P("subj", "ha", "dev"), P("subj", "ha", "dev"), P("subj", None, None, None))
    return jax.shard_map(
        per_device,
        mesh=mesh,
        in_specs=placed,
        out_specs=placed,
        check_vma=False,
    )
```

```python
import functools
import math

import jax
import jax.numpy as jnp
import ml_dtypes
import numpy as np
from jax import lax
from jax.experimental import pallas as pl
from jax.experimental.pallas import tpu as pltpu
from jax.sharding import PartitionSpec as P

STEPS = 4
STEP_SIZE = 4.0
STIFFNESS = 2.0
HALO = 2 * STEPS
LANES = 128
SUB = 8
F32 = jnp.float32
BF16 = jnp.bfloat16


def wavenumbers(modes):
    column = np.arange(modes)
    return np.where(column <= modes // 2, column, column - modes // 2)


def fourier_table(positions, length, modes):
    column = np.arange(modes)
    angles = (positions[:, None] * wavenumbers(modes)[None, :] % length) * (2.0 * math.pi / length)
    table = np.where(column[None, :] <= modes // 2, np.cos(angles), np.sin(angles))
    inside = (positions >= 0) & (positions < length)
    return np.where(inside[:, None], table, 0.0)


def mode_factor(planes, height, depth, modes_x, modes_yz):
    def terms(length, modes):
        eigen = 2.0 - 2.0 * np.cos(wavenumbers(modes) * (2.0 * math.pi / length))
        return eigen, np.where(np.arange(modes) == 0, length, length / 2.0)

    ex, wx = terms(planes, modes_x)
    ey, wy = terms(height, modes_yz)
    ez, wz = terms(depth, modes_yz)
    eigen = ex[:, None, None] + ey[None, :, None] + ez[None, None, :]
    norm = wx[:, None, None] * wy[None, :, None] * wz[None, None, :]
    count = modes_x * modes_yz * modes_yz
    return STEP_SIZE * math.sqrt(count) / (norm * np.square(1.0 + STIFFNESS * eigen))


def split_np(table):
    high = table.astype(np.float32).astype(ml_dtypes.bfloat16)
    low = (table - high.astype(np.float64)).astype(ml_dtypes.bfloat16)
    return high, low


class Sizes:
    def __init__(self, planes, rows, depth, modes_x, modes, count_height, count_depth):
        self.planes, self.rows, self.depth = planes, rows, depth
        self.modes_x, self.modes = modes_x, modes
        self.count_height, self.count_depth = count_height, count_depth
        self.tall = rows + 2 * HALO
        self.phases = -(-(depth + 2 * HALO) // LANES)
        self.wide = self.phases * LANES
        self.groups = planes // SUB
        self.tiles = depth // LANES
        self.packs = LANES // modes
        self.pairs = modes_x * modes
        self.chunk = self.pairs // self.packs
        assert planes % SUB == 0 and depth % LANES == 0 and rows % HALO == 0
        assert self.packs == 4 and self.wide >= depth + 2 * HALO

    def tables(self):
        n = self
        order_x = np.array([n.groups * s + g for g in range(n.groups) for s in range(SUB)])
        order_z = np.array([n.phases * l + s for s in range(n.phases) for l in range(LANES)])
        table_x = fourier_table(order_x, n.planes, n.modes_x)
        height, depth = n.rows * n.count_height, n.depth * n.count_depth
        bx = np.repeat(table_x, n.modes, axis=1) / math.sqrt(n.pairs * n.modes)
        by, by_t, bz_e, bz_p = [], [], [], []
        for i in range(n.count_height):
            table_y = fourier_table(np.arange(n.tall) - HALO + i * n.rows, height, n.modes)
            by.append(np.tile(table_y, (1, n.modes_x)))
            own = table_y[HALO : HALO + n.rows]
            by_t.append(np.repeat(own.T, n.planes, axis=1))
        bx_t = np.tile(table_x.T, (1, n.rows))
        for i in range(n.count_depth):
            place = order_z - HALO
            reach = (place >= -HALO) & (place < n.depth + HALO)
            table_z = fourier_table(place + i * n.depth, depth, n.modes) * reach[:, None]
            high, low = split_np(table_z.T)
            bz_e.append(np.concatenate([high, high, low, np.zeros_like(low)]))
            own = ((place >= 0) & (place < n.depth))[:, None]
            high, low = split_np(0.5 * table_z * own)
            held = np.zeros((3, n.wide, 2 * LANES), ml_dtypes.bfloat16)
            for c in range(3):
                held[c, :, n.modes * c : n.modes * (c + 1)] = high
                held[c, :, LANES + n.modes * c : LANES + n.modes * (c + 1)] = low
            bz_p.append(held)
        spread = np.zeros((n.depth + LANES, n.wide), ml_dtypes.bfloat16)
        for column, position in enumerate(order_z):
            z = position - HALO
            if 0 <= z < n.depth:
                spread[z, column] = 1
            elif -HALO <= z < 0:
                spread[n.depth + LANES + z, column] = 1
            elif n.depth <= z < n.depth + HALO:
                spread[z, column] = 1
        gather = np.ascontiguousarray(spread[: n.depth].T)
        factor = mode_factor(n.planes, height, depth, n.modes_x, n.modes)
        factor = factor.reshape(n.packs, n.chunk, n.modes).transpose(1, 0, 2).reshape(n.chunk, LANES)
        return dict(
            bx=bx.astype(np.float32),
            by=np.stack(by).astype(np.float32),
            bx_t=bx_t.astype(np.float32),
            by_t=np.stack(by_t).astype(np.float32),
            bz_e=np.stack(bz_e),
            bz_p=np.stack(bz_p),
            spread=spread,
            gather=gather,
            factor=factor.astype(np.float32),
        )


def split(value):
    high = value.astype(BF16)
    return high, (value - high.astype(F32)).astype(BF16)


def dot(a, b):
    return jnp.dot(a, b, preferred_element_type=F32)


def unpacked(packed, c, n):
    lane = lax.broadcasted_iota(jnp.int32, (n.chunk, LANES), 1) // n.modes
    piece = packed[c * n.chunk : (c + 1) * n.chunk]
    parts = []
    for g in range(n.packs):
        held = jnp.where(lane == g, piece, 0.0)
        held = held + pltpu.roll(held, n.modes, 1)
        parts.append(held + pltpu.roll(held, 2 * n.modes, 1))
    return jnp.concatenate(parts, axis=0)


def expand_into(n, coeffs, w_ref, bx_ref, by_ref, bz_ref, speed):
    for c in range(3):
        high, low = split(coeffs[c])
        w_ref[:, c * LANES : (c + 1) * LANES] = high
        w_ref[:, (3 + c) * LANES : (4 + c) * LANES] = low
    chunk = SUB
    lane = lax.broadcasted_iota(jnp.int32, (chunk * n.planes, LANES), 1) // n.modes

    def body(i, _):
        rows = pl.ds(pl.multiple_of(i * chunk, chunk), chunk)
        by = by_ref[rows, :]
        bx = bx_ref[...]
        table = jnp.concatenate([bx * by[j : j + 1, :] for j in range(chunk)], axis=0)
        high, low = split(table)
        main = dot(high, w_ref[...])
        rest = dot(low, w_ref[:, : 3 * LANES])
        size = None
        for c in range(3):
            inner = (
                main[:, c * LANES : (c + 1) * LANES]
                + main[:, (3 + c) * LANES : (4 + c) * LANES]
                + rest[:, c * LANES : (c + 1) * LANES]
            )
            head = inner.astype(BF16).astype(F32)
            mixed = jnp.where(lane == 1, inner - head, head).astype(BF16)
            full = dot(mixed, bz_ref[...])
            size = jnp.abs(full) if c == 0 else size + jnp.abs(full)
            for s in range(n.phases):
                part = full[:, s * LANES : (s + 1) * LANES]
                speed[c, rows, s] = part.reshape(chunk, n.groups, SUB, LANES)
        for s in range(n.phases):
            part = 1.0 - size[:, s * LANES : (s + 1) * LANES]
            speed[3, rows, s] = part.reshape(chunk, n.groups, SUB, LANES)
        return 0

    lax.fori_loop(0, n.tall // chunk, body, 0)


def own_copies(n, own, side, raw, sems):
    jobs = [(own.at[:, t * LANES : (t + 1) * LANES], raw.at[t]) for t in range(n.tiles)]
    jobs.append((side, raw.at[n.tiles]))
    return [pltpu.make_async_copy(a, b, sems.at[i]) for i, (a, b) in enumerate(jobs)]


def spread_rows(n, pick, spread, field, target, rows):
    columns = []
    for t in range(n.tiles + 1):
        blocks = [pick(t, j, g) for j in range(rows) for g in range(n.groups)]
        columns.append(jnp.concatenate(blocks, axis=0))
    value = jnp.concatenate(columns, axis=1)
    high, low = split(value)
    out = dot(high, spread[...]) + dot(low, spread[...])
    for s in range(n.phases):
        part = out[:, s * LANES : (s + 1) * LANES]
        field[target, s] = part.reshape(rows, n.groups, SUB, LANES)


def side_mask(n, place):
    left_half = lax.broadcasted_iota(jnp.int32, (SUB, LANES), 1) < LANES // 2
    right = jnp.where(place[1] < n.count_depth - 1, 1.0, 0.0)
    left = jnp.where(place[1] > 0, 1.0, 0.0)
    return jnp.where(left_half, right, left)


def spread_own(n, place, raw, spread, field):
    mask = side_mask(n, place)

    def body(i, _):
        y = pl.multiple_of(i * HALO, HALO)

        def pick(t, j, g):
            value = raw[t, pl.ds(g * n.rows + y + j, SUB, stride=n.groups * n.rows), :]
            return value * mask if t == n.tiles else value

        spread_rows(n, pick, spread, field, pl.ds(y + HALO, HALO), HALO)
        return 0

    lax.fori_loop(0, n.rows // HALO, body, 0)


def halo_copies(n, low, high, side_low, side_high, thin, sems):
    count = n.planes * HALO
    jobs = []
    for which, (rows, side) in enumerate(((low, side_low), (high, side_high))):
        for t in range(n.tiles):
            cut = rows.at[0:count, t * LANES : (t + 1) * LANES]
            jobs.append((cut, thin.at[t, which]))
        jobs.append((side, thin.at[n.tiles, which]))
    return [pltpu.make_async_copy(a, b, sems.at[i]) for i, (a, b) in enumerate(jobs)]


def spread_halos(n, place, thin, spread, field):
    mask = side_mask(n, place)
    for which, first in ((0, 0), (1, HALO + n.rows)):

        def pick(t, j, g):
            value = thin[t, which, pl.ds(g * HALO + j, SUB, stride=n.groups * HALO), :]
            return value * mask if t == n.tiles else value

        spread_rows(n, pick, spread, field, slice(first, first + HALO), HALO)


def edge_copies(n, low, high, thin, sems):
    count = n.planes * HALO
    jobs = []
    for which, rows in enumerate((low, high)):
        for t in range(n.tiles):
            cut = rows.at[count : count + n.planes, t * LANES : (t + 1) * LANES]
            jobs.append((cut, thin.at[t, which]))
    return [pltpu.make_async_copy(a, b, sems.at[i]) for i, (a, b) in enumerate(jobs)]


def spread_edges(n, thin, spread, image):
    blank = jnp.zeros((SUB, LANES), F32)
    for which, row in ((0, HALO - 1), (1, HALO + n.rows)):

        def pick(t, j, g):
            if t == n.tiles:
                return blank
            return thin[t, which, pl.ds(g, SUB, stride=n.groups), :]

        spread_rows(n, pick, spread, image, slice(row, row + 1), 1)


def neighbours(n, field, y0, rows):
    held = {}
    sub = lax.broadcasted_iota(jnp.int32, (SUB, LANES), 0)
    first, last = sub == 0, sub == SUB - 1
    phases, groups = n.phases, n.groups

    def at(j, s, g):
        if (j, s, g) not in held:
            held[j, s, g] = field[y0 + j, s, g]
        return held[j, s, g]

    edges = {}
    for j in range(rows):
        for g in range(groups):
            edges["zp", j, g] = pltpu.roll(at(j, 0, g), LANES - 1, 1)
            edges["zm", j, g] = pltpu.roll(at(j, phases - 1, g), 1, 1)
        for s in range(phases):
            edges["xp", j, s] = jnp.where(last, 0.0, pltpu.roll(at(j, s, 0), SUB - 1, 0))
            edges["xm", j, s] = jnp.where(first, 0.0, pltpu.roll(at(j, s, groups - 1), 1, 0))

    def around(j, s, g):
        xm = at(j, s, g - 1) if g else edges["xm", j, s]
        xp = at(j, s, g + 1) if g < groups - 1 else edges["xp", j, s]
        zm = at(j, s - 1, g) if s else edges["zm", j, g]
        zp = at(j, s + 1, g) if s < phases - 1 else edges["zp", j, g]
        return at(j, s, g), (xm, at(j - 1, s, g), zm), (xp, at(j + 1, s, g), zp)

    return around


def upwind_rows(n, source, target, speed, y0, rows, second):
    around = neighbours(n, source, y0, rows)
    for j in range(rows):
        for s in range(n.phases):
            for g in range(n.groups):
                here, behind, ahead = around(j, s, g)
                total = speed[3, y0 + j, s, g] * here
                for d in range(3):
                    u = speed[d, y0 + j, s, g]
                    total = total + jnp.abs(u) * jnp.where(u > 0, behind[d], ahead[d])
                if second:
                    total = 0.5 * (target[y0 + j, s, g] + total)
                target[y0 + j, s, g] = total


def sweep(n, source, target, speed, low, high, second):
    count = (high - low) // 4
    lax.fori_loop(
        0,
        count,
        lambda i, _: (upwind_rows(n, source, target, speed, low + 4 * i, 4, second), 0)[1],
        0,
    )
    return low + 4 * count


def stretch(n, source, target, speed, low, high, second, size):
    done = sweep(n, source, target, speed, low, high, second)
    if size % 4:
        upwind_rows(n, source, target, speed, done, size % 4, second)


def transport(n, field, spare, speed, start, stop):
    size = stop - start

    def step(r, _):
        k = 2 * r + 1
        stretch(n, field, spare, speed, start + k, stop - k, False, size - 2)
        stretch(n, spare, field, speed, start + k + 1, stop - k - 1, True, size)
        return 0

    lax.fori_loop(0, STEPS, step, 0)


def transport_edges(n, field, spare, speed):
    far = n.rows + HALO

    def step(r, _):
        k = 2 * r + 1
        for k, source, target, second in ((k, field, spare, False), (k + 1, spare, field, True)):
            for first in (k, far - k):
                for part in range(0, HALO, 4):
                    upwind_rows(n, source, target, speed, first + part, 4, second)
        return 0

    lax.fori_loop(0, STEPS, step, 0)


def deinterleave(n, field, gather, out):
    def body(i, _):
        y = pl.multiple_of(i * HALO, HALO)
        columns = [
            field[pl.ds(y + HALO, HALO), s].reshape(HALO * n.planes, LANES) for s in range(n.phases)
        ]
        high, low = split(jnp.concatenate(columns, axis=1))
        value = dot(high, gather[...]) + dot(low, gather[...])
        for t in range(n.tiles):
            for j in range(HALO):
                for g in range(n.groups):
                    row = j * n.planes + g * SUB
                    out[t, pl.ds(g * n.rows + y + j, SUB, stride=n.groups * n.rows), :] = value[
                        row : row + SUB, t * LANES : (t + 1) * LANES
                    ]
        return 0

    lax.fori_loop(0, n.rows // HALO, body, 0)


def result_copies(n, out, target, sems):
    return [
        pltpu.make_async_copy(out.at[t], target.at[:, t * LANES : (t + 1) * LANES], sems.at[t])
        for t in range(n.tiles)
    ]


def force(n, adjoint, image, f_high, f_low):
    def body(y, _):
        around = neighbours(n, image, y + HALO, 1)
        for s in range(n.phases):
            pieces = [[], [], []]
            for g in range(n.groups):
                _, behind, ahead = around(0, s, g)
                end = adjoint[y + HALO, s, g]
                for d in range(3):
                    pieces[d].append(end * (ahead[d] - behind[d]))
            for d in range(3):
                high, low = split(jnp.concatenate(pieces[d], axis=0))
                rows = pl.ds(pl.multiple_of(y * n.planes, n.planes), n.planes)
                f_high[d, rows, s * LANES : (s + 1) * LANES] = high
                f_low[d, rows, s * LANES : (s + 1) * LANES] = low
        return 0

    lax.fori_loop(0, n.rows, body, 0)


def project(n, f_high, f_low, bz_ref, bx_ref, by_ref, total, packed):
    size = HALO * n.planes
    total[...] = jnp.zeros_like(total)

    def body(i, _):
        start = pl.multiple_of(i * size, size)
        rows = pl.ds(start, size)
        main, rest = None, None
        for d in range(3):
            one = dot(f_high[d, rows, :], bz_ref[d])
            two = dot(f_low[d, rows, :], bz_ref[d, :, :LANES])
            main = one if d == 0 else main + one
            rest = two if d == 0 else rest + two
        inner = main[:, :LANES] + main[:, LANES:] + rest
        high, low = split(inner)
        by = by_ref[:, rows]
        bx = bx_ref[:, rows]
        table = jnp.concatenate([by * bx[a : a + 1, :] for a in range(n.modes_x)], axis=0)
        t_high, t_low = split(table)
        both = dot(t_high, jnp.concatenate([high, low], axis=1))
        total[...] += both[:, :LANES] + both[:, LANES:] + dot(t_low, high)
        return 0

    lax.fori_loop(0, n.rows // HALO, body, 0)
    lane = lax.broadcasted_iota(jnp.int32, (n.chunk, LANES), 1) // n.modes
    for c in range(3):
        value = jnp.zeros((n.chunk, LANES), F32)
        for g in range(n.packs):
            piece = total[g * n.chunk : (g + 1) * n.chunk, :]
            shift = (n.modes * (g - c)) % LANES
            value = jnp.where(lane == g, pltpu.roll(piece, shift, 1) if shift else piece, value)
        packed[c * n.chunk : (c + 1) * n.chunk, :] = value


def table_copies(place, pairs, sems):
    return [
        pltpu.make_async_copy(table.at[place[axis]], held, sems.at[i])
        for i, (table, axis, held) in enumerate(pairs)
    ]


def started(copies):
    for copy in copies:
        copy.start()
    return copies


def waited(copies):
    for copy in copies:
        copy.wait()


def own_modes(n, modes, c):
    return jnp.concatenate([modes[c]] * n.packs, axis=1)


def edge_rows(n, source, target, sems):
    far = n.rows
    spans = ((0, 2 * HALO), (far, far + 2 * HALO)) if far > HALO else ((0, n.tall),)
    return [
        pltpu.make_async_copy(source.at[c, p:q], target.at[c, p:q], sems.at[i, c])
        for i, (p, q) in enumerate(spans)
        for c in range(4)
    ]


def block_rows(n, sources, targets, sems):
    own = slice(HALO, HALO + n.rows)
    return [
        pltpu.make_async_copy(a.at[own], b.at[own], sems.at[i])
        for i, (a, b) in enumerate(zip(sources, targets, strict=True))
    ]


def inner_kernel(n, place, modes, bx, by, bz_e, spread, own_a, side_a, own_b, side_b, *rest):
    speed_out, field_out, spare_out, image_out, *rest = rest
    speed, field, spare, image, raw_a, raw_b, w, by_own, bz_own, sems, sems_t, sems_s, sems_f = rest
    tables = started(table_copies(place, ((by, 0, by_own), (bz_e, 1, bz_own)), sems_t))
    pulls_a = started(own_copies(n, own_a, side_a, raw_a, sems.at[0]))
    pulls_b = started(own_copies(n, own_b, side_b, raw_b, sems.at[1]))
    coeffs = [-own_modes(n, modes, c) for c in range(3)]
    waited(tables)
    expand_into(n, coeffs, w, bx, by_own, bz_own, speed)
    pushes = started(edge_rows(n, speed, speed_out, sems_s))
    waited(pulls_a)
    spread_own(n, place, raw_a, spread, field)
    transport(n, field, spare, speed, HALO, HALO + n.rows)
    pushes += started(block_rows(n, (field, spare), (field_out, spare_out), sems_f))
    waited(pulls_b)
    spread_own(n, place, raw_b, spread, image)
    pushes += started(block_rows(n, (image,), (image_out,), sems_f.at[2:3]))
    waited(pushes)


def outer_kernel(n, place, speed_in, field_in, spare_in, image_in, spread, gather, bx_t, *rest):
    by_t, bz_p, low, high, side_low, side_high, packed, end, *rest = rest
    speed, field, spare, image, *rest = rest
    raw, thin, edge, f_high, f_low, total, by_own, bz_own, *rest = rest
    sems_h, sems_e, sems_o, sems_t, sems_s, sems_f = rest
    pulls = started(halo_copies(n, low, high, side_low, side_high, thin, sems_h))
    speeds = started(edge_rows(n, speed_in, speed, sems_s))
    fields = started(block_rows(n, (field_in, spare_in), (field, spare), sems_f))
    images = started(block_rows(n, (image_in,), (image,), sems_f.at[2:3]))
    edges = started(edge_copies(n, low, high, edge, sems_e))
    tables = started(table_copies(place, ((by_t, 0, by_own), (bz_p, 1, bz_own)), sems_t))
    waited(pulls)
    spread_halos(n, place, thin, spread, field)
    waited(speeds + fields)
    transport_edges(n, field, spare, speed)
    deinterleave(n, field, gather, raw)
    pushes = started(result_copies(n, raw, end, sems_o))
    waited(edges + images)
    spread_edges(n, edge, spread, image)
    force(n, field, image, f_high, f_low)
    waited(tables)
    project(n, f_high, f_low, bz_own, bx_t, by_own, total, packed)
    waited(pushes)


def last_kernel(n, place, modes, summed, factor, bx, by, bz_e, spread, gather, *rest):
    image, low, high, side_low, side_high, end, updated, *rest = rest
    speed, field, spare, raw, thin, w, by_own, bz_own, sems_h, sems_o, sems_t, sems_f = rest
    tables = started(table_copies(place, ((by, 0, by_own), (bz_e, 1, bz_own)), sems_t))
    pulls = started(halo_copies(n, low, high, side_low, side_high, thin, sems_h))
    images = started(block_rows(n, (image,), (field,), sems_f))
    scale = jnp.concatenate([factor[...]] * 3, axis=0)
    packed = scale * summed[...]
    coeffs = [own_modes(n, modes, c) + unpacked(packed, c, n) for c in range(3)]
    for c in range(3):
        updated[c] = coeffs[c][:, : n.modes]
    waited(tables)
    expand_into(n, coeffs, w, bx, by_own, bz_own, speed)
    waited(pulls + images)
    spread_halos(n, place, thin, spread, field)
    transport(n, field, spare, speed, 0, n.tall)
    deinterleave(n, field, gather, raw)
    waited(started(result_copies(n, raw, end, sems_o)))


def swap_with(value, axis, step):
    count = lax.axis_size(axis)
    return lax.ppermute(value, axis, [(i, i ^ step) for i in range(count)])


def sum_over_devices(packed):
    count_height, count_depth = lax.axis_size("ha"), lax.axis_size("dev")
    if count_depth != 2 or count_height & (count_height - 1):
        return lax.psum(packed, ("ha", "dev"))
    halves = packed.reshape(2, -1, LANES)
    side = lax.axis_index("dev")
    kept = lax.dynamic_index_in_dim(halves, side, 0, False)
    given = lax.dynamic_index_in_dim(halves, 1 - side, 0, False)
    kept = kept + swap_with(given, "dev", 1)
    step = 1
    while step < count_height:
        kept = kept + swap_with(kept, "ha", step)
        step *= 2
    other = swap_with(kept, "dev", 1)
    first = jnp.where(side == 0, kept, other)
    second = jnp.where(side == 0, other, kept)
    return jnp.concatenate([first, second], axis=0)


def beside(cells):
    count = lax.axis_size("dev")
    depth = cells.shape[-1]
    if count == 1:
        return cells[..., :LANES]
    if count == 2:
        start = jnp.where(lax.axis_index("dev") == 0, depth - LANES, 0)
        return swap_with(lax.dynamic_slice_in_dim(cells, start, LANES, cells.ndim - 1), "dev", 1)
    lane = lax.broadcasted_iota(jnp.int32, (1,) * (cells.ndim - 1) + (LANES,), cells.ndim - 1)
    ends = range(count - 1)
    from_left = lax.ppermute(cells[..., -LANES:], "dev", [(i, i + 1) for i in ends])
    from_right = lax.ppermute(cells[..., :LANES], "dev", [(i + 1, i) for i in ends])
    return jnp.where(lane < LANES // 2, from_right, from_left)


def to_neighbours(last_rows, first_rows):
    ends = range(lax.axis_size("ha") - 1)
    low = lax.ppermute(last_rows, "ha", [(i, i + 1) for i in ends])
    high = lax.ppermute(first_rows, "ha", [(i + 1, i) for i in ends])
    return low, high


def corners(low, high, count):
    both = beside(jnp.concatenate([low[:count], high[:count]], axis=0))
    return both[:count], both[count:]


def per_device(brain_image, adjoint_field, velocity_modes):
    planes, rows, depth = brain_image.shape
    n = Sizes(
        planes,
        rows,
        depth,
        velocity_modes.shape[1],
        velocity_modes.shape[2],
        lax.axis_size("ha"),
        lax.axis_size("dev"),
    )
    t = {name: jnp.asarray(value) for name, value in n.tables().items()}
    place = jnp.stack([lax.axis_index("ha"), lax.axis_index("dev")]).astype(jnp.int32)
    modes = velocity_modes.reshape(3, n.pairs, n.modes)
    flat = (planes * rows, depth)
    thin_count = planes * HALO

    def rows_sent(cells):
        return cells.reshape(-1, depth)

    side_a = beside(adjoint_field).reshape(-1, LANES)
    side_b = beside(brain_image).reshape(-1, LANES)
    low_a, high_a = to_neighbours(
        jnp.concatenate([rows_sent(adjoint_field[:, -HALO:]), brain_image[:, -1]], axis=0),
        jnp.concatenate([rows_sent(adjoint_field[:, :HALO]), brain_image[:, 0]], axis=0),
    )

    held = pl.BlockSpec(memory_space=pltpu.VMEM)
    small = pl.BlockSpec(memory_space=pltpu.SMEM)
    outside = pl.BlockSpec(memory_space=pl.ANY)
    block = (n.tall, n.phases, n.groups, SUB, LANES)
    field_shape = jax.ShapeDtypeStruct(block, F32)
    speed_shape = jax.ShapeDtypeStruct((4,) + block, F32)
    raw = pltpu.VMEM((n.tiles + 1, planes * rows, LANES), F32)
    thin = pltpu.VMEM((n.tiles + 1, 2, thin_count, LANES), F32)
    weights = pltpu.VMEM((n.pairs, 6 * LANES), BF16)
    semaphores = pltpu.SemaphoreType.DMA
    by_own = pltpu.VMEM(t["by"].shape[1:], F32)
    bz_own = pltpu.VMEM(t["bz_e"].shape[1:], BF16)

    def params(mebibytes):
        return pltpu.CompilerParams(vmem_limit_bytes=mebibytes * 2**20)

    def cost(us):
        return pl.CostEstimate(flops=int(us * 1e9), bytes_accessed=int(us * 3e6), transcendentals=0)

    blocks = [pltpu.VMEM(block, F32)] * 3
    speeds = pltpu.VMEM((4,) + block, F32)
    speed, field, spare, image = pl.pallas_call(
        functools.partial(inner_kernel, n),
        in_specs=[small, held, held, outside, outside, held] + [outside] * 4,
        out_specs=[outside] * 4,
        out_shape=[speed_shape, field_shape, field_shape, field_shape],
        scratch_shapes=[
            speeds, *blocks, raw, raw, weights, by_own, bz_own,
            semaphores((2, n.tiles + 1)), semaphores((2,)), semaphores((2, 4)), semaphores((3,)),
        ],
        compiler_params=params(40),
        cost_estimate=cost(20),
    )(
        place, modes, t["bx"], t["by"], t["bz_e"], t["spread"], adjoint_field.reshape(flat), side_a,
        brain_image.reshape(flat), side_b,
    )

    sent_b = (rows_sent(brain_image[:, -HALO:]), rows_sent(brain_image[:, :HALO]))
    low_a, high_a, last_b, first_b, field = lax.optimization_barrier(
        (low_a, high_a, *sent_b, field)
    )
    corner_a = corners(low_a, high_a, thin_count)
    low_b, high_b = to_neighbours(last_b, first_b)

    packed, adjoint_end = pl.pallas_call(
        functools.partial(outer_kernel, n),
        in_specs=[small] + [outside] * 4 + [held] * 3 + [outside] * 6,
        out_specs=[held, outside],
        out_shape=[
            jax.ShapeDtypeStruct((3 * n.chunk, LANES), F32),
            jax.ShapeDtypeStruct(flat, F32),
        ],
        scratch_shapes=[
            speeds,
            *blocks,
            raw,
            thin,
            pltpu.VMEM((n.tiles, 2, planes, LANES), F32),
            pltpu.VMEM((3, planes * rows, n.wide), BF16),
            pltpu.VMEM((3, planes * rows, n.wide), BF16),
            pltpu.VMEM((n.pairs, LANES), F32),
            pltpu.VMEM(t["by_t"].shape[1:], F32),
            pltpu.VMEM(t["bz_p"].shape[1:], BF16),
            semaphores((2 * n.tiles + 2,)),
            semaphores((2 * n.tiles,)),
            semaphores((n.tiles,)),
            semaphores((2,)),
            semaphores((2, 4)),
            semaphores((3,)),
        ],
        compiler_params=params(44),
        cost_estimate=cost(16),
    )(
        place, speed, field, spare, image, t["spread"], t["gather"], t["bx_t"], t["by_t"], t["bz_p"],
        low_a, high_a, *corner_a,
    )
    packed, low_b, high_b = lax.optimization_barrier((packed, low_b, high_b))
    summed = sum_over_devices(packed)
    corner_b = corners(low_b, high_b, thin_count)
    image_end, updated = pl.pallas_call(
        functools.partial(last_kernel, n),
        in_specs=[small, held, held, held, held, outside, outside, held, held] + [outside] * 5,
        out_specs=[outside, held],
        out_shape=[
            jax.ShapeDtypeStruct(flat, F32),
            jax.ShapeDtypeStruct((3, n.pairs, n.modes), F32),
        ],
        scratch_shapes=[
            speeds,
            *blocks[:2],
            raw,
            thin,
            weights,
            by_own,
            bz_own,
            semaphores((2 * n.tiles + 2,)),
            semaphores((n.tiles,)),
            semaphores((2,)),
            semaphores((1,)),
        ],
        compiler_params=params(40),
        cost_estimate=cost(28),
    )(
        place, modes, summed, t["factor"], t["bx"], t["by"], t["bz_e"], t["spread"], t["gather"],
        image, low_b, high_b, *corner_b,
    )
    return (
        adjoint_end.reshape(brain_image.shape),
        image_end.reshape(brain_image.shape),
        updated.reshape(velocity_modes.shape),
    )


def solution(mesh):
    placed = (P("subj", "ha", "dev"), P("subj", "ha", "dev"), P("subj", None, None, None))
    return jax.shard_map(
        per_device,
        mesh=mesh,
        in_specs=placed,
        out_specs=placed,
        check_vma=False,
    )
```

```python
import functools
import math

import jax
import jax.numpy as jnp
import ml_dtypes
import numpy as np
from jax import lax
from jax.experimental import pallas as pl
from jax.experimental.pallas import tpu as pltpu
from jax.sharding import PartitionSpec as P

STEPS = 4
STEP_SIZE = 4.0
STIFFNESS = 2.0
HALO = 2 * STEPS
LANES = 128
SUB = 8
F32 = jnp.float32
BF16 = jnp.bfloat16


def wavenumbers(modes):
    column = np.arange(modes)
    return np.where(column <= modes // 2, column, column - modes // 2)


def fourier_table(positions, length, modes):
    column = np.arange(modes)
    angles = (positions[:, None] * wavenumbers(modes)[None, :] % length) * (2.0 * math.pi / length)
    table = np.where(column[None, :] <= modes // 2, np.cos(angles), np.sin(angles))
    inside = (positions >= 0) & (positions < length)
    return np.where(inside[:, None], table, 0.0)


def mode_factor(planes, height, depth, modes_x, modes_yz):
    def terms(length, modes):
        eigen = 2.0 - 2.0 * np.cos(wavenumbers(modes) * (2.0 * math.pi / length))
        return eigen, np.where(np.arange(modes) == 0, length, length / 2.0)

    ex, wx = terms(planes, modes_x)
    ey, wy = terms(height, modes_yz)
    ez, wz = terms(depth, modes_yz)
    eigen = ex[:, None, None] + ey[None, :, None] + ez[None, None, :]
    norm = wx[:, None, None] * wy[None, :, None] * wz[None, None, :]
    count = modes_x * modes_yz * modes_yz
    return STEP_SIZE * math.sqrt(count) / (norm * np.square(1.0 + STIFFNESS * eigen))


def split_np(table):
    high = table.astype(np.float32).astype(ml_dtypes.bfloat16)
    low = (table - high.astype(np.float64)).astype(ml_dtypes.bfloat16)
    return high, low


class Sizes:
    def __init__(self, planes, rows, depth, modes_x, modes, count_height, count_depth):
        self.planes, self.rows, self.depth = planes, rows, depth
        self.modes_x, self.modes = modes_x, modes
        self.count_height, self.count_depth = count_height, count_depth
        self.tall = rows + 2 * HALO
        self.phases = -(-(depth + 2 * HALO) // LANES)
        self.wide = self.phases * LANES
        self.groups = planes // SUB
        self.tiles = depth // LANES
        self.packs = LANES // modes
        self.pairs = modes_x * modes
        self.chunk = self.pairs // self.packs
        assert planes % SUB == 0 and depth % LANES == 0 and rows % HALO == 0
        assert self.packs == 4 and self.wide >= depth + 2 * HALO

    def tables(self):
        n = self
        order_x = np.array([n.groups * s + g for g in range(n.groups) for s in range(SUB)])
        order_z = np.array([n.phases * l + s for s in range(n.phases) for l in range(LANES)])
        table_x = fourier_table(order_x, n.planes, n.modes_x)
        height, depth = n.rows * n.count_height, n.depth * n.count_depth
        bx = np.repeat(table_x, n.modes, axis=1) / math.sqrt(n.pairs * n.modes)
        by, by_t, bz_e, bz_p = [], [], [], []
        for i in range(n.count_height):
            table_y = fourier_table(np.arange(n.tall) - HALO + i * n.rows, height, n.modes)
            by.append(np.tile(table_y, (1, n.modes_x)))
            own = table_y[HALO : HALO + n.rows]
            by_t.append(np.repeat(own.T, n.planes, axis=1))
        bx_t = np.tile(table_x.T, (1, n.rows))
        for i in range(n.count_depth):
            place = order_z - HALO
            reach = (place >= -HALO) & (place < n.depth + HALO)
            table_z = fourier_table(place + i * n.depth, depth, n.modes) * reach[:, None]
            high, low = split_np(table_z.T)
            bz_e.append(np.concatenate([high, high, low, np.zeros_like(low)]))
            own = ((place >= 0) & (place < n.depth))[:, None]
            high, low = split_np(0.5 * table_z * own)
            held = np.zeros((3, n.wide, 2 * LANES), ml_dtypes.bfloat16)
            for c in range(3):
                held[c, :, n.modes * c : n.modes * (c + 1)] = high
                held[c, :, LANES + n.modes * c : LANES + n.modes * (c + 1)] = low
            bz_p.append(held)
        spread = np.zeros((n.depth + LANES, n.wide), ml_dtypes.bfloat16)
        for column, position in enumerate(order_z):
            z = position - HALO
            if 0 <= z < n.depth:
                spread[z, column] = 1
            elif -HALO <= z < 0:
                spread[n.depth + LANES + z, column] = 1
            elif n.depth <= z < n.depth + HALO:
                spread[z, column] = 1
        gather = np.ascontiguousarray(spread[: n.depth].T)
        factor = mode_factor(n.planes, height, depth, n.modes_x, n.modes)
        factor = factor.reshape(n.packs, n.chunk, n.modes).transpose(1, 0, 2).reshape(n.chunk, LANES)
        return dict(
            bx=bx.astype(np.float32),
            by=np.stack(by).astype(np.float32),
            bx_t=bx_t.astype(np.float32),
            by_t=np.stack(by_t).astype(np.float32),
            bz_e=np.stack(bz_e),
            bz_p=np.stack(bz_p),
            spread=spread,
            gather=gather,
            factor=factor.astype(np.float32),
        )


def split(value):
    high = value.astype(BF16)
    return high, (value - high.astype(F32)).astype(BF16)


def dot(a, b):
    return jnp.dot(a, b, preferred_element_type=F32)


def unpacked(packed, c, n):
    lane = lax.broadcasted_iota(jnp.int32, (n.chunk, LANES), 1) // n.modes
    piece = packed[c * n.chunk : (c + 1) * n.chunk]
    parts = []
    for g in range(n.packs):
        held = jnp.where(lane == g, piece, 0.0)
        held = held + pltpu.roll(held, n.modes, 1)
        parts.append(held + pltpu.roll(held, 2 * n.modes, 1))
    return jnp.concatenate(parts, axis=0)


def expand_into(n, coeffs, w_ref, bx_ref, by_ref, bz_ref, speed):
    for c in range(3):
        high, low = split(coeffs[c])
        w_ref[:, c * LANES : (c + 1) * LANES] = high
        w_ref[:, (3 + c) * LANES : (4 + c) * LANES] = low
    chunk = SUB
    lane = lax.broadcasted_iota(jnp.int32, (chunk * n.planes, LANES), 1) // n.modes

    def body(i, _):
        rows = pl.ds(pl.multiple_of(i * chunk, chunk), chunk)
        by = by_ref[rows, :]
        bx = bx_ref[...]
        table = jnp.concatenate([bx * by[j : j + 1, :] for j in range(chunk)], axis=0)
        high, low = split(table)
        main = dot(high, w_ref[...])
        rest = dot(low, w_ref[:, : 3 * LANES])
        size = None
        for c in range(3):
            inner = (
                main[:, c * LANES : (c + 1) * LANES]
                + main[:, (3 + c) * LANES : (4 + c) * LANES]
                + rest[:, c * LANES : (c + 1) * LANES]
            )
            head = inner.astype(BF16).astype(F32)
            mixed = jnp.where(lane == 1, inner - head, head).astype(BF16)
            full = dot(mixed, bz_ref[...])
            size = jnp.abs(full) if c == 0 else size + jnp.abs(full)
            for s in range(n.phases):
                part = full[:, s * LANES : (s + 1) * LANES]
                speed[c, rows, s] = part.reshape(chunk, n.groups, SUB, LANES)
        for s in range(n.phases):
            part = 1.0 - size[:, s * LANES : (s + 1) * LANES]
            speed[3, rows, s] = part.reshape(chunk, n.groups, SUB, LANES)
        return 0

    lax.fori_loop(0, n.tall // chunk, body, 0)


def own_copies(n, own, side, raw, sems):
    jobs = [(own.at[:, t * LANES : (t + 1) * LANES], raw.at[t]) for t in range(n.tiles)]
    jobs.append((side, raw.at[n.tiles]))
    return [pltpu.make_async_copy(a, b, sems.at[i]) for i, (a, b) in enumerate(jobs)]


def spread_rows(n, pick, spread, field, target, rows):
    columns = []
    for t in range(n.tiles + 1):
        blocks = [pick(t, j, g) for j in range(rows) for g in range(n.groups)]
        columns.append(jnp.concatenate(blocks, axis=0))
    value = jnp.concatenate(columns, axis=1)
    high, low = split(value)
    out = dot(high, spread[...]) + dot(low, spread[...])
    for s in range(n.phases):
        part = out[:, s * LANES : (s + 1) * LANES]
        field[target, s] = part.reshape(rows, n.groups, SUB, LANES)


def side_mask(n, place):
    left_half = lax.broadcasted_iota(jnp.int32, (SUB, LANES), 1) < LANES // 2
    right = jnp.where(place[1] < n.count_depth - 1, 1.0, 0.0)
    left = jnp.where(place[1] > 0, 1.0, 0.0)
    return jnp.where(left_half, right, left)


def spread_own(n, place, raw, spread, field):
    mask = side_mask(n, place)

    def body(i, _):
        y = pl.multiple_of(i * HALO, HALO)

        def pick(t, j, g):
            value = raw[t, pl.ds(g * n.rows + y + j, SUB, stride=n.groups * n.rows), :]
            return value * mask if t == n.tiles else value

        spread_rows(n, pick, spread, field, pl.ds(y + HALO, HALO), HALO)
        return 0

    lax.fori_loop(0, n.rows // HALO, body, 0)


def halo_copies(n, low, high, side_low, side_high, thin, sems):
    count = n.planes * HALO
    jobs = []
    for which, (rows, side) in enumerate(((low, side_low), (high, side_high))):
        for t in range(n.tiles):
            cut = rows.at[0:count, t * LANES : (t + 1) * LANES]
            jobs.append((cut, thin.at[t, which]))
        jobs.append((side, thin.at[n.tiles, which]))
    return [pltpu.make_async_copy(a, b, sems.at[i]) for i, (a, b) in enumerate(jobs)]


def spread_halos(n, place, thin, spread, field):
    mask = side_mask(n, place)
    for which, first in ((0, 0), (1, HALO + n.rows)):

        def pick(t, j, g):
            value = thin[t, which, pl.ds(g * HALO + j, SUB, stride=n.groups * HALO), :]
            return value * mask if t == n.tiles else value

        spread_rows(n, pick, spread, field, slice(first, first + HALO), HALO)


def edge_copies(n, low, high, thin, sems):
    count = n.planes * HALO
    jobs = []
    for which, rows in enumerate((low, high)):
        for t in range(n.tiles):
            cut = rows.at[count : count + n.planes, t * LANES : (t + 1) * LANES]
            jobs.append((cut, thin.at[t, which]))
    return [pltpu.make_async_copy(a, b, sems.at[i]) for i, (a, b) in enumerate(jobs)]


def spread_edges(n, thin, spread, image):
    blank = jnp.zeros((SUB, LANES), F32)
    for which, row in ((0, HALO - 1), (1, HALO + n.rows)):

        def pick(t, j, g):
            if t == n.tiles:
                return blank
            return thin[t, which, pl.ds(g, SUB, stride=n.groups), :]

        spread_rows(n, pick, spread, image, slice(row, row + 1), 1)


def neighbours(n, field, y0, rows):
    held = {}
    sub = lax.broadcasted_iota(jnp.int32, (SUB, LANES), 0)
    first, last = sub == 0, sub == SUB - 1
    phases, groups = n.phases, n.groups

    def at(j, s, g):
        if (j, s, g) not in held:
            held[j, s, g] = field[y0 + j, s, g]
        return held[j, s, g]

    edges = {}
    for j in range(rows):
        for g in range(groups):
            edges["zp", j, g] = pltpu.roll(at(j, 0, g), LANES - 1, 1)
            edges["zm", j, g] = pltpu.roll(at(j, phases - 1, g), 1, 1)
        for s in range(phases):
            edges["xp", j, s] = jnp.where(last, 0.0, pltpu.roll(at(j, s, 0), SUB - 1, 0))
            edges["xm", j, s] = jnp.where(first, 0.0, pltpu.roll(at(j, s, groups - 1), 1, 0))

    def around(j, s, g):
        xm = at(j, s, g - 1) if g else edges["xm", j, s]
        xp = at(j, s, g + 1) if g < groups - 1 else edges["xp", j, s]
        zm = at(j, s - 1, g) if s else edges["zm", j, g]
        zp = at(j, s + 1, g) if s < phases - 1 else edges["zp", j, g]
        return at(j, s, g), (xm, at(j - 1, s, g), zm), (xp, at(j + 1, s, g), zp)

    return around


def upwind_rows(n, source, target, speed, y0, rows, second):
    around = neighbours(n, source, y0, rows)
    for j in range(rows):
        for s in range(n.phases):
            for g in range(n.groups):
                here, behind, ahead = around(j, s, g)
                total = speed[3, y0 + j, s, g] * here
                for d in range(3):
                    u = speed[d, y0 + j, s, g]
                    total = total + jnp.abs(u) * jnp.where(u > 0, behind[d], ahead[d])
                if second:
                    total = 0.5 * (target[y0 + j, s, g] + total)
                target[y0 + j, s, g] = total


def sweep(n, source, target, speed, low, high, second):
    count = (high - low) // 4
    lax.fori_loop(
        0,
        count,
        lambda i, _: (upwind_rows(n, source, target, speed, low + 4 * i, 4, second), 0)[1],
        0,
    )
    return low + 4 * count


def stretch(n, source, target, speed, low, high, second, size):
    done = sweep(n, source, target, speed, low, high, second)
    if size % 4:
        upwind_rows(n, source, target, speed, done, size % 4, second)


def transport(n, field, spare, speed, start, stop):
    size = stop - start

    def step(r, _):
        k = 2 * r + 1
        stretch(n, field, spare, speed, start + k, stop - k, False, size - 2)
        stretch(n, spare, field, speed, start + k + 1, stop - k - 1, True, size)
        return 0

    lax.fori_loop(0, STEPS, step, 0)


def transport_edges(n, field, spare, speed):
    far = n.rows + HALO

    def step(r, _):
        k = 2 * r + 1
        for k, source, target, second in ((k, field, spare, False), (k + 1, spare, field, True)):
            for first in (k, far - k):
                for part in range(0, HALO, 4):
                    upwind_rows(n, source, target, speed, first + part, 4, second)
        return 0

    lax.fori_loop(0, STEPS, step, 0)


def deinterleave(n, field, gather, out):
    def body(i, _):
        y = pl.multiple_of(i * HALO, HALO)
        columns = [
            field[pl.ds(y + HALO, HALO), s].reshape(HALO * n.planes, LANES) for s in range(n.phases)
        ]
        high, low = split(jnp.concatenate(columns, axis=1))
        value = dot(high, gather[...]) + dot(low, gather[...])
        for t in range(n.tiles):
            for j in range(HALO):
                for g in range(n.groups):
                    row = j * n.planes + g * SUB
                    out[t, pl.ds(g * n.rows + y + j, SUB, stride=n.groups * n.rows), :] = value[
                        row : row + SUB, t * LANES : (t + 1) * LANES
                    ]
        return 0

    lax.fori_loop(0, n.rows // HALO, body, 0)


def result_copies(n, out, target, sems):
    return [
        pltpu.make_async_copy(out.at[t], target.at[:, t * LANES : (t + 1) * LANES], sems.at[t])
        for t in range(n.tiles)
    ]


def force(n, adjoint, image, f_high, f_low):
    def body(y, _):
        around = neighbours(n, image, y + HALO, 1)
        for s in range(n.phases):
            pieces = [[], [], []]
            for g in range(n.groups):
                _, behind, ahead = around(0, s, g)
                end = adjoint[y + HALO, s, g]
                for d in range(3):
                    pieces[d].append(end * (ahead[d] - behind[d]))
            for d in range(3):
                high, low = split(jnp.concatenate(pieces[d], axis=0))
                rows = pl.ds(pl.multiple_of(y * n.planes, n.planes), n.planes)
                f_high[d, rows, s * LANES : (s + 1) * LANES] = high
                f_low[d, rows, s * LANES : (s + 1) * LANES] = low
        return 0

    lax.fori_loop(0, n.rows, body, 0)


def project(n, f_high, f_low, bz_ref, bx_ref, by_ref, total, packed):
    size = HALO * n.planes
    total[...] = jnp.zeros_like(total)

    def body(i, _):
        start = pl.multiple_of(i * size, size)
        rows = pl.ds(start, size)
        main, rest = None, None
        for d in range(3):
            one = dot(f_high[d, rows, :], bz_ref[d])
            two = dot(f_low[d, rows, :], bz_ref[d, :, :LANES])
            main = one if d == 0 else main + one
            rest = two if d == 0 else rest + two
        inner = main[:, :LANES] + main[:, LANES:] + rest
        high, low = split(inner)
        by = by_ref[:, rows]
        bx = bx_ref[:, rows]
        table = jnp.concatenate([by * bx[a : a + 1, :] for a in range(n.modes_x)], axis=0)
        t_high, t_low = split(table)
        both = dot(t_high, jnp.concatenate([high, low], axis=1))
        total[...] += both[:, :LANES] + both[:, LANES:] + dot(t_low, high)
        return 0

    lax.fori_loop(0, n.rows // HALO, body, 0)
    lane = lax.broadcasted_iota(jnp.int32, (n.chunk, LANES), 1) // n.modes
    for c in range(3):
        value = jnp.zeros((n.chunk, LANES), F32)
        for g in range(n.packs):
            piece = total[g * n.chunk : (g + 1) * n.chunk, :]
            shift = (n.modes * (g - c)) % LANES
            value = jnp.where(lane == g, pltpu.roll(piece, shift, 1) if shift else piece, value)
        packed[c * n.chunk : (c + 1) * n.chunk, :] = value


def table_copies(place, pairs, sems):
    return [
        pltpu.make_async_copy(table.at[place[axis]], held, sems.at[i])
        for i, (table, axis, held) in enumerate(pairs)
    ]


def started(copies):
    for copy in copies:
        copy.start()
    return copies


def waited(copies):
    for copy in copies:
        copy.wait()


def own_modes(n, modes, c):
    return jnp.concatenate([modes[c]] * n.packs, axis=1)


def edge_rows(n, source, target, sems):
    far = n.rows
    spans = ((0, 2 * HALO), (far, far + 2 * HALO)) if far > HALO else ((0, n.tall),)
    return [
        pltpu.make_async_copy(source.at[c, p:q], target.at[c, p:q], sems.at[i, c])
        for i, (p, q) in enumerate(spans)
        for c in range(4)
    ]


def block_rows(n, sources, targets, sems):
    own = slice(HALO, HALO + n.rows)
    return [
        pltpu.make_async_copy(a.at[own], b.at[own], sems.at[i])
        for i, (a, b) in enumerate(zip(sources, targets, strict=True))
    ]


def inner_kernel(n, place, modes, bx, by, bz_e, spread, own_a, side_a, own_b, side_b, *rest):
    speed_out, field_out, spare_out, image_out, *rest = rest
    speed, field, spare, image, raw_a, raw_b, w, by_own, bz_own, sems, sems_t, sems_s, sems_f = rest
    tables = started(table_copies(place, ((by, 0, by_own), (bz_e, 1, bz_own)), sems_t))
    pulls_a = started(own_copies(n, own_a, side_a, raw_a, sems.at[0]))
    pulls_b = started(own_copies(n, own_b, side_b, raw_b, sems.at[1]))
    coeffs = [-own_modes(n, modes, c) for c in range(3)]
    waited(tables)
    expand_into(n, coeffs, w, bx, by_own, bz_own, speed)
    pushes = started(edge_rows(n, speed, speed_out, sems_s))
    waited(pulls_a)
    spread_own(n, place, raw_a, spread, field)
    transport(n, field, spare, speed, HALO, HALO + n.rows)
    pushes += started(block_rows(n, (field, spare), (field_out, spare_out), sems_f))
    waited(pulls_b)
    spread_own(n, place, raw_b, spread, image)
    pushes += started(block_rows(n, (image,), (image_out,), sems_f.at[2:3]))
    waited(pushes)


def outer_kernel(n, place, speed_in, field_in, spare_in, image_in, spread, gather, bx_t, *rest):
    by_t, bz_p, low, high, side_low, side_high, packed, end, *rest = rest
    speed, field, spare, image, *rest = rest
    raw, thin, edge, f_high, f_low, total, by_own, bz_own, *rest = rest
    sems_h, sems_e, sems_o, sems_t, sems_s, sems_f = rest
    pulls = started(halo_copies(n, low, high, side_low, side_high, thin, sems_h))
    speeds = started(edge_rows(n, speed_in, speed, sems_s))
    fields = started(block_rows(n, (field_in, spare_in), (field, spare), sems_f))
    images = started(block_rows(n, (image_in,), (image,), sems_f.at[2:3]))
    edges = started(edge_copies(n, low, high, edge, sems_e))
    tables = started(table_copies(place, ((by_t, 0, by_own), (bz_p, 1, bz_own)), sems_t))
    waited(pulls)
    spread_halos(n, place, thin, spread, field)
    waited(speeds + fields)
    transport_edges(n, field, spare, speed)
    deinterleave(n, field, gather, raw)
    pushes = started(result_copies(n, raw, end, sems_o))
    waited(edges + images)
    spread_edges(n, edge, spread, image)
    force(n, field, image, f_high, f_low)
    waited(tables)
    project(n, f_high, f_low, bz_own, bx_t, by_own, total, packed)
    waited(pushes)


def last_kernel(n, place, modes, summed, factor, bx, by, bz_e, spread, gather, *rest):
    image, low, high, side_low, side_high, end, updated, *rest = rest
    speed, field, spare, raw, thin, w, by_own, bz_own, sems_h, sems_o, sems_t, sems_f = rest
    tables = started(table_copies(place, ((by, 0, by_own), (bz_e, 1, bz_own)), sems_t))
    pulls = started(halo_copies(n, low, high, side_low, side_high, thin, sems_h))
    images = started(block_rows(n, (image,), (field,), sems_f))
    scale = jnp.concatenate([factor[...]] * 3, axis=0)
    packed = scale * summed[...]
    coeffs = [own_modes(n, modes, c) + unpacked(packed, c, n) for c in range(3)]
    for c in range(3):
        updated[c] = coeffs[c][:, : n.modes]
    waited(tables)
    expand_into(n, coeffs, w, bx, by_own, bz_own, speed)
    waited(pulls + images)
    spread_halos(n, place, thin, spread, field)
    transport(n, field, spare, speed, 0, n.tall)
    deinterleave(n, field, gather, raw)
    waited(started(result_copies(n, raw, end, sems_o)))


def swap_with(value, axis, step):
    count = lax.axis_size(axis)
    return lax.ppermute(value, axis, [(i, i ^ step) for i in range(count)])


def sum_over_devices(packed):
    count_height, count_depth = lax.axis_size("ha"), lax.axis_size("dev")
    if count_depth != 2 or count_height & (count_height - 1):
        return lax.psum(packed, ("ha", "dev"))
    halves = packed.reshape(2, -1, LANES)
    side = lax.axis_index("dev")
    kept = lax.dynamic_index_in_dim(halves, side, 0, False)
    given = lax.dynamic_index_in_dim(halves, 1 - side, 0, False)
    kept = kept + swap_with(given, "dev", 1)
    step = 1
    while step < count_height:
        kept = kept + swap_with(kept, "ha", step)
        step *= 2
    other = swap_with(kept, "dev", 1)
    first = jnp.where(side == 0, kept, other)
    second = jnp.where(side == 0, other, kept)
    return jnp.concatenate([first, second], axis=0)


def beside(cells):
    count = lax.axis_size("dev")
    depth = cells.shape[-1]
    if count == 1:
        return cells[..., :LANES]
    if count == 2:
        start = jnp.where(lax.axis_index("dev") == 0, depth - LANES, 0)
        return swap_with(lax.dynamic_slice_in_dim(cells, start, LANES, cells.ndim - 1), "dev", 1)
    lane = lax.broadcasted_iota(jnp.int32, (1,) * (cells.ndim - 1) + (LANES,), cells.ndim - 1)
    ends = range(count - 1)
    from_left = lax.ppermute(cells[..., -LANES:], "dev", [(i, i + 1) for i in ends])
    from_right = lax.ppermute(cells[..., :LANES], "dev", [(i + 1, i) for i in ends])
    return jnp.where(lane < LANES // 2, from_right, from_left)


def to_neighbours(last_rows, first_rows):
    ends = range(lax.axis_size("ha") - 1)
    low = lax.ppermute(last_rows, "ha", [(i, i + 1) for i in ends])
    high = lax.ppermute(first_rows, "ha", [(i + 1, i) for i in ends])
    return low, high


def corners(low, high, count):
    both = beside(jnp.concatenate([low[:count], high[:count]], axis=0))
    return both[:count], both[count:]


def per_device(brain_image, adjoint_field, velocity_modes):
    planes, rows, depth = brain_image.shape
    n = Sizes(
        planes,
        rows,
        depth,
        velocity_modes.shape[1],
        velocity_modes.shape[2],
        lax.axis_size("ha"),
        lax.axis_size("dev"),
    )
    t = {name: jnp.asarray(value) for name, value in n.tables().items()}
    place = jnp.stack([lax.axis_index("ha"), lax.axis_index("dev")]).astype(jnp.int32)
    modes = velocity_modes.reshape(3, n.pairs, n.modes)
    flat = (planes * rows, depth)
    thin_count = planes * HALO

    def rows_sent(cells):
        return cells.reshape(-1, depth)

    side_a = beside(adjoint_field).reshape(-1, LANES)
    side_b = beside(brain_image).reshape(-1, LANES)
    low_a, high_a = to_neighbours(
        jnp.concatenate([rows_sent(adjoint_field[:, -HALO:]), brain_image[:, -1]], axis=0),
        jnp.concatenate([rows_sent(adjoint_field[:, :HALO]), brain_image[:, 0]], axis=0),
    )

    held = pl.BlockSpec(memory_space=pltpu.VMEM)
    small = pl.BlockSpec(memory_space=pltpu.SMEM)
    outside = pl.BlockSpec(memory_space=pl.ANY)
    block = (n.tall, n.phases, n.groups, SUB, LANES)
    field_shape = jax.ShapeDtypeStruct(block, F32)
    speed_shape = jax.ShapeDtypeStruct((4,) + block, F32)
    raw = pltpu.VMEM((n.tiles + 1, planes * rows, LANES), F32)
    thin = pltpu.VMEM((n.tiles + 1, 2, thin_count, LANES), F32)
    weights = pltpu.VMEM((n.pairs, 6 * LANES), BF16)
    semaphores = pltpu.SemaphoreType.DMA
    by_own = pltpu.VMEM(t["by"].shape[1:], F32)
    bz_own = pltpu.VMEM(t["bz_e"].shape[1:], BF16)

    def params(mebibytes):
        return pltpu.CompilerParams(vmem_limit_bytes=mebibytes * 2**20)

    def cost(us):
        return pl.CostEstimate(flops=int(us * 1e9), bytes_accessed=int(us * 3e6), transcendentals=0)

    blocks = [pltpu.VMEM(block, F32)] * 3
    speeds = pltpu.VMEM((4,) + block, F32)
    speed, field, spare, image = pl.pallas_call(
        functools.partial(inner_kernel, n),
        in_specs=[small, held, held, outside, outside, held] + [outside] * 4,
        out_specs=[outside] * 4,
        out_shape=[speed_shape, field_shape, field_shape, field_shape],
        scratch_shapes=[
            speeds, *blocks, raw, raw, weights, by_own, bz_own,
            semaphores((2, n.tiles + 1)), semaphores((2,)), semaphores((2, 4)), semaphores((3,)),
        ],
        compiler_params=params(60),
        cost_estimate=cost(20),
    )(
        place, modes, t["bx"], t["by"], t["bz_e"], t["spread"], adjoint_field.reshape(flat), side_a,
        brain_image.reshape(flat), side_b,
    )

    sent_b = (rows_sent(brain_image[:, -HALO:]), rows_sent(brain_image[:, :HALO]))
    low_a, high_a, last_b, first_b, field = lax.optimization_barrier(
        (low_a, high_a, *sent_b, field)
    )
    corner_a = corners(low_a, high_a, thin_count)
    low_b, high_b = to_neighbours(last_b, first_b)

    packed, adjoint_end = pl.pallas_call(
        functools.partial(outer_kernel, n),
        in_specs=[small] + [outside] * 4 + [held] * 3 + [outside] * 6,
        out_specs=[held, outside],
        out_shape=[
            jax.ShapeDtypeStruct((3 * n.chunk, LANES), F32),
            jax.ShapeDtypeStruct(flat, F32),
        ],
        scratch_shapes=[
            speeds,
            *blocks,
            raw,
            thin,
            pltpu.VMEM((n.tiles, 2, planes, LANES), F32),
            pltpu.VMEM((3, planes * rows, n.wide), BF16),
            pltpu.VMEM((3, planes * rows, n.wide), BF16),
            pltpu.VMEM((n.pairs, LANES), F32),
            pltpu.VMEM(t["by_t"].shape[1:], F32),
            pltpu.VMEM(t["bz_p"].shape[1:], BF16),
            semaphores((2 * n.tiles + 2,)),
            semaphores((2 * n.tiles,)),
            semaphores((n.tiles,)),
            semaphores((2,)),
            semaphores((2, 4)),
            semaphores((3,)),
        ],
        compiler_params=params(60),
        cost_estimate=cost(16),
    )(
        place, speed, field, spare, image, t["spread"], t["gather"], t["bx_t"], t["by_t"], t["bz_p"],
        low_a, high_a, *corner_a,
    )
    packed, low_b, high_b = lax.optimization_barrier((packed, low_b, high_b))
    summed = sum_over_devices(packed)
    corner_b = corners(low_b, high_b, thin_count)
    image_end, updated = pl.pallas_call(
        functools.partial(last_kernel, n),
        in_specs=[small, held, held, held, held, outside, outside, held, held] + [outside] * 5,
        out_specs=[outside, held],
        out_shape=[
            jax.ShapeDtypeStruct(flat, F32),
            jax.ShapeDtypeStruct((3, n.pairs, n.modes), F32),
        ],
        scratch_shapes=[
            speeds,
            *blocks[:2],
            raw,
            thin,
            weights,
            by_own,
            bz_own,
            semaphores((2 * n.tiles + 2,)),
            semaphores((n.tiles,)),
            semaphores((2,)),
            semaphores((1,)),
        ],
        compiler_params=params(60),
        cost_estimate=cost(28),
    )(
        place, modes, summed, t["factor"], t["bx"], t["by"], t["bz_e"], t["spread"], t["gather"],
        image, low_b, high_b, *corner_b,
    )
    return (
        adjoint_end.reshape(brain_image.shape),
        image_end.reshape(brain_image.shape),
        updated.reshape(velocity_modes.shape),
    )


def solution(mesh):
    placed = (P("subj", "ha", "dev"), P("subj", "ha", "dev"), P("subj", None, None, None))
    return jax.shard_map(
        per_device,
        mesh=mesh,
        in_specs=placed,
        out_specs=placed,
        check_vma=False,
    )
```

```python
import functools
import math

import jax
import jax.numpy as jnp
import ml_dtypes
import numpy as np
from jax import lax
from jax.experimental import pallas as pl
from jax.experimental.pallas import tpu as pltpu
from jax.sharding import PartitionSpec as P

STEPS = 4
STEP_SIZE = 4.0
STIFFNESS = 2.0
HALO = 2 * STEPS
LANES = 128
SUB = 8
F32 = jnp.float32
BF16 = jnp.bfloat16


def wavenumbers(modes):
    column = np.arange(modes)
    return np.where(column <= modes // 2, column, column - modes // 2)


def fourier_table(positions, length, modes):
    column = np.arange(modes)
    angles = (positions[:, None] * wavenumbers(modes)[None, :] % length) * (2.0 * math.pi / length)
    table = np.where(column[None, :] <= modes // 2, np.cos(angles), np.sin(angles))
    inside = (positions >= 0) & (positions < length)
    return np.where(inside[:, None], table, 0.0)


def mode_factor(planes, height, depth, modes_x, modes_yz):
    def terms(length, modes):
        eigen = 2.0 - 2.0 * np.cos(wavenumbers(modes) * (2.0 * math.pi / length))
        return eigen, np.where(np.arange(modes) == 0, length, length / 2.0)

    ex, wx = terms(planes, modes_x)
    ey, wy = terms(height, modes_yz)
    ez, wz = terms(depth, modes_yz)
    eigen = ex[:, None, None] + ey[None, :, None] + ez[None, None, :]
    norm = wx[:, None, None] * wy[None, :, None] * wz[None, None, :]
    count = modes_x * modes_yz * modes_yz
    return STEP_SIZE * math.sqrt(count) / (norm * np.square(1.0 + STIFFNESS * eigen))


def split_np(table):
    high = table.astype(np.float32).astype(ml_dtypes.bfloat16)
    low = (table - high.astype(np.float64)).astype(ml_dtypes.bfloat16)
    return high, low


class Sizes:
    def __init__(self, planes, rows, depth, modes_x, modes, count_height, count_depth):
        self.planes, self.rows, self.depth = planes, rows, depth
        self.modes_x, self.modes = modes_x, modes
        self.count_height, self.count_depth = count_height, count_depth
        self.tall = rows + 2 * HALO
        self.phases = -(-(depth + 2 * HALO) // LANES)
        self.wide = self.phases * LANES
        self.groups = planes // SUB
        self.tiles = depth // LANES
        self.packs = LANES // modes
        self.pairs = modes_x * modes
        self.chunk = self.pairs // self.packs
        assert planes % SUB == 0 and depth % LANES == 0 and rows % HALO == 0
        assert self.packs == 4 and self.wide >= depth + 2 * HALO

    def tables(self):
        n = self
        order_x = np.array([n.groups * s + g for g in range(n.groups) for s in range(SUB)])
        order_z = np.array([n.phases * l + s for s in range(n.phases) for l in range(LANES)])
        table_x = fourier_table(order_x, n.planes, n.modes_x)
        height, depth = n.rows * n.count_height, n.depth * n.count_depth
        bx = np.repeat(table_x, n.modes, axis=1) / math.sqrt(n.pairs * n.modes)
        by, by_t, bz_e, bz_p = [], [], [], []
        for i in range(n.count_height):
            table_y = fourier_table(np.arange(n.tall) - HALO + i * n.rows, height, n.modes)
            by.append(np.tile(table_y, (1, n.modes_x)))
            own = table_y[HALO : HALO + n.rows]
            by_t.append(np.repeat(own.T, n.planes, axis=1))
        bx_t = np.tile(table_x.T, (1, n.rows))
        for i in range(n.count_depth):
            place = order_z - HALO
            reach = (place >= -HALO) & (place < n.depth + HALO)
            table_z = fourier_table(place + i * n.depth, depth, n.modes) * reach[:, None]
            high, low = split_np(table_z.T)
            bz_e.append(np.concatenate([high, high, low, np.zeros_like(low)]))
            own = ((place >= 0) & (place < n.depth))[:, None]
            high, low = split_np(0.5 * table_z * own)
            held = np.zeros((3, n.wide, 2 * LANES), ml_dtypes.bfloat16)
            for c in range(3):
                held[c, :, n.modes * c : n.modes * (c + 1)] = high
                held[c, :, LANES + n.modes * c : LANES + n.modes * (c + 1)] = low
            bz_p.append(held)
        spread = np.zeros((n.depth + LANES, n.wide), ml_dtypes.bfloat16)
        for column, position in enumerate(order_z):
            z = position - HALO
            if 0 <= z < n.depth:
                spread[z, column] = 1
            elif -HALO <= z < 0:
                spread[n.depth + LANES + z, column] = 1
            elif n.depth <= z < n.depth + HALO:
                spread[z, column] = 1
        gather = np.ascontiguousarray(spread[: n.depth].T)
        factor = mode_factor(n.planes, height, depth, n.modes_x, n.modes)
        factor = factor.reshape(n.packs, n.chunk, n.modes).transpose(1, 0, 2).reshape(n.chunk, LANES)
        return dict(
            bx=bx.astype(np.float32),
            by=np.stack(by).astype(np.float32),
            bx_t=bx_t.astype(np.float32),
            by_t=np.stack(by_t).astype(np.float32),
            bz_e=np.stack(bz_e),
            bz_p=np.stack(bz_p),
            spread=spread,
            gather=gather,
            factor=factor.astype(np.float32),
        )


def split(value):
    high = value.astype(BF16)
    return high, (value - high.astype(F32)).astype(BF16)


def dot(a, b):
    return jnp.dot(a, b, preferred_element_type=F32)


def unpacked(packed, c, n):
    lane = lax.broadcasted_iota(jnp.int32, (n.chunk, LANES), 1) // n.modes
    piece = packed[c * n.chunk : (c + 1) * n.chunk]
    parts = []
    for g in range(n.packs):
        held = jnp.where(lane == g, piece, 0.0)
        held = held + pltpu.roll(held, n.modes, 1)
        parts.append(held + pltpu.roll(held, 2 * n.modes, 1))
    return jnp.concatenate(parts, axis=0)


def expand_into(n, coeffs, w_ref, bx_ref, by_ref, bz_ref, speed):
    for c in range(3):
        high, low = split(coeffs[c])
        w_ref[:, c * LANES : (c + 1) * LANES] = high
        w_ref[:, (3 + c) * LANES : (4 + c) * LANES] = low
    chunk = SUB
    lane = lax.broadcasted_iota(jnp.int32, (chunk * n.planes, LANES), 1) // n.modes

    def body(i, _):
        rows = pl.ds(pl.multiple_of(i * chunk, chunk), chunk)
        by = by_ref[rows, :]
        bx = bx_ref[...]
        table = jnp.concatenate([bx * by[j : j + 1, :] for j in range(chunk)], axis=0)
        high, low = split(table)
        main = dot(high, w_ref[...])
        rest = dot(low, w_ref[:, : 3 * LANES])
        size = None
        for c in range(3):
            inner = (
                main[:, c * LANES : (c + 1) * LANES]
                + main[:, (3 + c) * LANES : (4 + c) * LANES]
                + rest[:, c * LANES : (c + 1) * LANES]
            )
            head = inner.astype(BF16).astype(F32)
            mixed = jnp.where(lane == 1, inner - head, head).astype(BF16)
            full = dot(mixed, bz_ref[...])
            size = jnp.abs(full) if c == 0 else size + jnp.abs(full)
            for s in range(n.phases):
                part = full[:, s * LANES : (s + 1) * LANES]
                speed[c, rows, s] = part.reshape(chunk, n.groups, SUB, LANES)
        for s in range(n.phases):
            part = 1.0 - size[:, s * LANES : (s + 1) * LANES]
            speed[3, rows, s] = part.reshape(chunk, n.groups, SUB, LANES)
        return 0

    lax.fori_loop(0, n.tall // chunk, body, 0)


def own_copies(n, own, side, raw, sems):
    jobs = [(own.at[:, t * LANES : (t + 1) * LANES], raw.at[t]) for t in range(n.tiles)]
    jobs.append((side, raw.at[n.tiles]))
    return [pltpu.make_async_copy(a, b, sems.at[i]) for i, (a, b) in enumerate(jobs)]


def spread_rows(n, pick, spread, field, target, rows):
    columns = []
    for t in range(n.tiles + 1):
        blocks = [pick(t, j, g) for j in range(rows) for g in range(n.groups)]
        columns.append(jnp.concatenate(blocks, axis=0))
    value = jnp.concatenate(columns, axis=1)
    high, low = split(value)
    out = dot(high, spread[...]) + dot(low, spread[...])
    for s in range(n.phases):
        part = out[:, s * LANES : (s + 1) * LANES]
        field[target, s] = part.reshape(rows, n.groups, SUB, LANES)


def side_mask(n, place):
    left_half = lax.broadcasted_iota(jnp.int32, (SUB, LANES), 1) < LANES // 2
    right = jnp.where(place[1] < n.count_depth - 1, 1.0, 0.0)
    left = jnp.where(place[1] > 0, 1.0, 0.0)
    return jnp.where(left_half, right, left)


def spread_own(n, place, raw, spread, field):
    mask = side_mask(n, place)

    def body(i, _):
        y = pl.multiple_of(i * HALO, HALO)

        def pick(t, j, g):
            value = raw[t, pl.ds(g * n.rows + y + j, SUB, stride=n.groups * n.rows), :]
            return value * mask if t == n.tiles else value

        spread_rows(n, pick, spread, field, pl.ds(y + HALO, HALO), HALO)
        return 0

    lax.fori_loop(0, n.rows // HALO, body, 0)


def halo_copies(n, low, high, side_low, side_high, thin, sems):
    count = n.planes * HALO
    jobs = []
    for which, (rows, side) in enumerate(((low, side_low), (high, side_high))):
        for t in range(n.tiles):
            cut = rows.at[0:count, t * LANES : (t + 1) * LANES]
            jobs.append((cut, thin.at[t, which]))
        jobs.append((side, thin.at[n.tiles, which]))
    return [pltpu.make_async_copy(a, b, sems.at[i]) for i, (a, b) in enumerate(jobs)]


def spread_halos(n, place, thin, spread, field):
    mask = side_mask(n, place)
    for which, first in ((0, 0), (1, HALO + n.rows)):

        def pick(t, j, g):
            value = thin[t, which, pl.ds(g * HALO + j, SUB, stride=n.groups * HALO), :]
            return value * mask if t == n.tiles else value

        spread_rows(n, pick, spread, field, slice(first, first + HALO), HALO)


def edge_copies(n, low, high, thin, sems):
    count = n.planes * HALO
    jobs = []
    for which, rows in enumerate((low, high)):
        for t in range(n.tiles):
            cut = rows.at[count : count + n.planes, t * LANES : (t + 1) * LANES]
            jobs.append((cut, thin.at[t, which]))
    return [pltpu.make_async_copy(a, b, sems.at[i]) for i, (a, b) in enumerate(jobs)]


def spread_edges(n, thin, spread, image):
    blank = jnp.zeros((SUB, LANES), F32)
    for which, row in ((0, HALO - 1), (1, HALO + n.rows)):

        def pick(t, j, g):
            if t == n.tiles:
                return blank
            return thin[t, which, pl.ds(g, SUB, stride=n.groups), :]

        spread_rows(n, pick, spread, image, slice(row, row + 1), 1)


def neighbours(n, field, y0, rows):
    held = {}
    sub = lax.broadcasted_iota(jnp.int32, (SUB, LANES), 0)
    first, last = sub == 0, sub == SUB - 1
    phases, groups = n.phases, n.groups

    def at(j, s, g):
        if (j, s, g) not in held:
            held[j, s, g] = field[y0 + j, s, g]
        return held[j, s, g]

    edges = {}
    for j in range(rows):
        for g in range(groups):
            edges["zp", j, g] = pltpu.roll(at(j, 0, g), LANES - 1, 1)
            edges["zm", j, g] = pltpu.roll(at(j, phases - 1, g), 1, 1)
        for s in range(phases):
            edges["xp", j, s] = jnp.where(last, 0.0, pltpu.roll(at(j, s, 0), SUB - 1, 0))
            edges["xm", j, s] = jnp.where(first, 0.0, pltpu.roll(at(j, s, groups - 1), 1, 0))

    def around(j, s, g):
        xm = at(j, s, g - 1) if g else edges["xm", j, s]
        xp = at(j, s, g + 1) if g < groups - 1 else edges["xp", j, s]
        zm = at(j, s - 1, g) if s else edges["zm", j, g]
        zp = at(j, s + 1, g) if s < phases - 1 else edges["zp", j, g]
        return at(j, s, g), (xm, at(j - 1, s, g), zm), (xp, at(j + 1, s, g), zp)

    return around


def upwind_rows(n, source, target, speed, y0, rows, second):
    around = neighbours(n, source, y0, rows)
    for j in range(rows):
        for s in range(n.phases):
            for g in range(n.groups):
                here, behind, ahead = around(j, s, g)
                total = speed[3, y0 + j, s, g] * here
                for d in range(3):
                    u = speed[d, y0 + j, s, g]
                    total = total + jnp.abs(u) * jnp.where(u > 0, behind[d], ahead[d])
                if second:
                    total = 0.5 * (target[y0 + j, s, g] + total)
                target[y0 + j, s, g] = total


def sweep(n, source, target, speed, low, high, second):
    count = (high - low) // 4
    lax.fori_loop(
        0,
        count,
        lambda i, _: (upwind_rows(n, source, target, speed, low + 4 * i, 4, second), 0)[1],
        0,
    )
    return low + 4 * count


def stretch(n, source, target, speed, low, high, second, size):
    done = sweep(n, source, target, speed, low, high, second)
    if size % 4:
        upwind_rows(n, source, target, speed, done, size % 4, second)


def transport(n, field, spare, speed, start, stop):
    size = stop - start

    def step(r, _):
        k = 2 * r + 1
        stretch(n, field, spare, speed, start + k, stop - k, False, size - 2)
        stretch(n, spare, field, speed, start + k + 1, stop - k - 1, True, size)
        return 0

    lax.fori_loop(0, STEPS, step, 0)


def transport_edges(n, field, spare, speed):
    far = n.rows + HALO

    def step(r, _):
        k = 2 * r + 1
        for k, source, target, second in ((k, field, spare, False), (k + 1, spare, field, True)):
            for first in (k, far - k):
                for part in range(0, HALO, 4):
                    upwind_rows(n, source, target, speed, first + part, 4, second)
        return 0

    lax.fori_loop(0, STEPS, step, 0)


def deinterleave(n, field, gather, out):
    def body(i, _):
        y = pl.multiple_of(i * HALO, HALO)
        columns = [
            field[pl.ds(y + HALO, HALO), s].reshape(HALO * n.planes, LANES) for s in range(n.phases)
        ]
        high, low = split(jnp.concatenate(columns, axis=1))
        value = dot(high, gather[...]) + dot(low, gather[...])
        for t in range(n.tiles):
            for j in range(HALO):
                for g in range(n.groups):
                    row = j * n.planes + g * SUB
                    out[t, pl.ds(g * n.rows + y + j, SUB, stride=n.groups * n.rows), :] = value[
                        row : row + SUB, t * LANES : (t + 1) * LANES
                    ]
        return 0

    lax.fori_loop(0, n.rows // HALO, body, 0)


def result_copies(n, out, target, sems):
    return [
        pltpu.make_async_copy(out.at[t], target.at[:, t * LANES : (t + 1) * LANES], sems.at[t])
        for t in range(n.tiles)
    ]


def force(n, adjoint, image, f_high, f_low):
    def body(y, _):
        around = neighbours(n, image, y + HALO, 1)
        for s in range(n.phases):
            pieces = [[], [], []]
            for g in range(n.groups):
                _, behind, ahead = around(0, s, g)
                end = adjoint[y + HALO, s, g]
                for d in range(3):
                    pieces[d].append(end * (ahead[d] - behind[d]))
            for d in range(3):
                high, low = split(jnp.concatenate(pieces[d], axis=0))
                rows = pl.ds(pl.multiple_of(y * n.planes, n.planes), n.planes)
                f_high[d, rows, s * LANES : (s + 1) * LANES] = high
                f_low[d, rows, s * LANES : (s + 1) * LANES] = low
        return 0

    lax.fori_loop(0, n.rows, body, 0)


def project(n, f_high, f_low, bz_ref, bx_ref, by_ref, total, packed):
    size = HALO * n.planes
    total[...] = jnp.zeros_like(total)

    def body(i, _):
        start = pl.multiple_of(i * size, size)
        rows = pl.ds(start, size)
        main, rest = None, None
        for d in range(3):
            one = dot(f_high[d, rows, :], bz_ref[d])
            two = dot(f_low[d, rows, :], bz_ref[d, :, :LANES])
            main = one if d == 0 else main + one
            rest = two if d == 0 else rest + two
        inner = main[:, :LANES] + main[:, LANES:] + rest
        high, low = split(inner)
        by = by_ref[:, rows]
        bx = bx_ref[:, rows]
        table = jnp.concatenate([by * bx[a : a + 1, :] for a in range(n.modes_x)], axis=0)
        t_high, t_low = split(table)
        both = dot(t_high, jnp.concatenate([high, low], axis=1))
        total[...] += both[:, :LANES] + both[:, LANES:] + dot(t_low, high)
        return 0

    lax.fori_loop(0, n.rows // HALO, body, 0)
    lane = lax.broadcasted_iota(jnp.int32, (n.chunk, LANES), 1) // n.modes
    for c in range(3):
        value = jnp.zeros((n.chunk, LANES), F32)
        for g in range(n.packs):
            piece = total[g * n.chunk : (g + 1) * n.chunk, :]
            shift = (n.modes * (g - c)) % LANES
            value = jnp.where(lane == g, pltpu.roll(piece, shift, 1) if shift else piece, value)
        packed[c * n.chunk : (c + 1) * n.chunk, :] = value


def table_copies(place, pairs, sems):
    return [
        pltpu.make_async_copy(table.at[place[axis]], held, sems.at[i])
        for i, (table, axis, held) in enumerate(pairs)
    ]


def started(copies):
    for copy in copies:
        copy.start()
    return copies


def waited(copies):
    for copy in copies:
        copy.wait()


def own_modes(n, modes, c):
    return jnp.concatenate([modes[c]] * n.packs, axis=1)


def edge_rows(n, source, target, sems):
    far = n.rows
    spans = ((0, 2 * HALO), (far, far + 2 * HALO)) if far > HALO else ((0, n.tall),)
    return [
        pltpu.make_async_copy(source.at[c, p:q], target.at[c, p:q], sems.at[i, c])
        for i, (p, q) in enumerate(spans)
        for c in range(4)
    ]


def block_rows(n, sources, targets, sems):
    own = slice(HALO, HALO + n.rows)
    return [
        pltpu.make_async_copy(a.at[own], b.at[own], sems.at[i])
        for i, (a, b) in enumerate(zip(sources, targets, strict=True))
    ]


def inner_kernel(n, place, modes, bx, by, bz_e, spread, own_a, side_a, own_b, side_b, *rest):
    speed_out, field_out, spare_out, image_out, *rest = rest
    speed, field, spare, image, raw_a, raw_b, w, by_own, bz_own, sems, sems_t, sems_s, sems_f = rest
    tables = started(table_copies(place, ((by, 0, by_own), (bz_e, 1, bz_own)), sems_t))
    pulls_a = started(own_copies(n, own_a, side_a, raw_a, sems.at[0]))
    pulls_b = started(own_copies(n, own_b, side_b, raw_b, sems.at[1]))
    coeffs = [-own_modes(n, modes, c) for c in range(3)]
    waited(tables)
    expand_into(n, coeffs, w, bx, by_own, bz_own, speed)
    pushes = started(edge_rows(n, speed, speed_out, sems_s))
    waited(pulls_a)
    spread_own(n, place, raw_a, spread, field)
    transport(n, field, spare, speed, HALO, HALO + n.rows)
    pushes += started(block_rows(n, (field, spare), (field_out, spare_out), sems_f))
    waited(pulls_b)
    spread_own(n, place, raw_b, spread, image)
    pushes += started(block_rows(n, (image,), (image_out,), sems_f.at[2:3]))
    waited(pushes)


def outer_kernel(n, place, speed_in, field_in, spare_in, image_in, spread, gather, bx_t, *rest):
    by_t, bz_p, low, high, side_low, side_high, kept, given, end, *rest = rest
    speed, field, spare, image, *rest = rest
    raw, thin, edge, f_high, f_low, total, by_own, bz_own, *rest = rest
    sems_h, sems_e, sems_o, sems_t, sems_s, sems_f, packed = rest
    pulls = started(halo_copies(n, low, high, side_low, side_high, thin, sems_h))
    speeds = started(edge_rows(n, speed_in, speed, sems_s))
    fields = started(block_rows(n, (field_in, spare_in), (field, spare), sems_f))
    images = started(block_rows(n, (image_in,), (image,), sems_f.at[2:3]))
    edges = started(edge_copies(n, low, high, edge, sems_e))
    tables = started(table_copies(place, ((by_t, 0, by_own), (bz_p, 1, bz_own)), sems_t))
    waited(pulls)
    spread_halos(n, place, thin, spread, field)
    waited(speeds + fields)
    transport_edges(n, field, spare, speed)
    deinterleave(n, field, gather, raw)
    pushes = started(result_copies(n, raw, end, sems_o))
    waited(edges + images)
    spread_edges(n, edge, spread, image)
    force(n, field, image, f_high, f_low)
    waited(tables)
    project(n, f_high, f_low, bz_own, bx_t, by_own, total, packed)
    half = packed.shape[0] // 2
    side = place[1] % 2
    kept[...] = packed[pl.ds(pl.multiple_of(side * half, half), half), :]
    given[...] = packed[pl.ds(pl.multiple_of((1 - side) * half, half), half), :]
    waited(pushes)


def last_kernel(n, place, modes, kept, other, factor, bx, by, bz_e, spread, gather, *rest):
    image, low, high, side_low, side_high, end, updated, *rest = rest
    speed, field, spare, raw, thin, w, by_own, bz_own, sems_h, sems_o, sems_t, sems_f = rest
    tables = started(table_copies(place, ((by, 0, by_own), (bz_e, 1, bz_own)), sems_t))
    pulls = started(halo_copies(n, low, high, side_low, side_high, thin, sems_h))
    images = started(block_rows(n, (image,), (field,), sems_f))
    scale = jnp.concatenate([factor[...]] * 3, axis=0)
    even = place[1] % 2 == 0
    first = jnp.where(even, kept[...], other[...])
    second = jnp.where(even, other[...], kept[...])
    packed = scale * jnp.concatenate([first, second], axis=0)
    coeffs = [own_modes(n, modes, c) + unpacked(packed, c, n) for c in range(3)]
    for c in range(3):
        updated[c] = coeffs[c][:, : n.modes]
    waited(tables)
    expand_into(n, coeffs, w, bx, by_own, bz_own, speed)
    waited(pulls + images)
    spread_halos(n, place, thin, spread, field)
    transport(n, field, spare, speed, 0, n.tall)
    deinterleave(n, field, gather, raw)
    waited(started(result_copies(n, raw, end, sems_o)))


def swap_with(value, axis, step):
    count = lax.axis_size(axis)
    return lax.ppermute(value, axis, [(i, i ^ step) for i in range(count)])


def sum_over_devices(kept, given):
    count_height, count_depth = lax.axis_size("ha"), lax.axis_size("dev")
    if count_depth != 2 or count_height & (count_height - 1):
        even = lax.axis_index("dev") % 2 == 0
        halves = jnp.stack([jnp.where(even, kept, given), jnp.where(even, given, kept)])
        halves = lax.psum(halves, ("ha", "dev"))
        return jnp.where(even, halves[0], halves[1]), jnp.where(even, halves[1], halves[0])
    kept = kept + swap_with(given, "dev", 1)
    step = 1
    while step < count_height:
        kept = kept + swap_with(kept, "ha", step)
        step *= 2
    return kept, swap_with(kept, "dev", 1)


def beside(cells):
    count = lax.axis_size("dev")
    depth = cells.shape[-1]
    if count == 1:
        return cells[..., :LANES]
    if count == 2:
        start = jnp.where(lax.axis_index("dev") == 0, depth - LANES, 0)
        return swap_with(lax.dynamic_slice_in_dim(cells, start, LANES, cells.ndim - 1), "dev", 1)
    lane = lax.broadcasted_iota(jnp.int32, (1,) * (cells.ndim - 1) + (LANES,), cells.ndim - 1)
    ends = range(count - 1)
    from_left = lax.ppermute(cells[..., -LANES:], "dev", [(i, i + 1) for i in ends])
    from_right = lax.ppermute(cells[..., :LANES], "dev", [(i + 1, i) for i in ends])
    return jnp.where(lane < LANES // 2, from_right, from_left)


def to_neighbours(last_rows, first_rows):
    ends = range(lax.axis_size("ha") - 1)
    low = lax.ppermute(last_rows, "ha", [(i, i + 1) for i in ends])
    high = lax.ppermute(first_rows, "ha", [(i + 1, i) for i in ends])
    return low, high


def corners(low, high, count):
    both = beside(jnp.concatenate([low[:count], high[:count]], axis=0))
    return both[:count], both[count:]


def per_device(brain_image, adjoint_field, velocity_modes):
    planes, rows, depth = brain_image.shape
    n = Sizes(
        planes,
        rows,
        depth,
        velocity_modes.shape[1],
        velocity_modes.shape[2],
        lax.axis_size("ha"),
        lax.axis_size("dev"),
    )
    t = {name: jnp.asarray(value) for name, value in n.tables().items()}
    place = jnp.stack([lax.axis_index("ha"), lax.axis_index("dev")]).astype(jnp.int32)
    modes = velocity_modes.reshape(3, n.pairs, n.modes)
    flat = (planes * rows, depth)
    thin_count = planes * HALO

    def rows_sent(cells):
        return cells.reshape(-1, depth)

    side_a = beside(adjoint_field).reshape(-1, LANES)
    side_b = beside(brain_image).reshape(-1, LANES)
    low_a, high_a = to_neighbours(
        jnp.concatenate([rows_sent(adjoint_field[:, -HALO:]), brain_image[:, -1]], axis=0),
        jnp.concatenate([rows_sent(adjoint_field[:, :HALO]), brain_image[:, 0]], axis=0),
    )

    held = pl.BlockSpec(memory_space=pltpu.VMEM)
    small = pl.BlockSpec(memory_space=pltpu.SMEM)
    outside = pl.BlockSpec(memory_space=pl.ANY)
    block = (n.tall, n.phases, n.groups, SUB, LANES)
    field_shape = jax.ShapeDtypeStruct(block, F32)
    speed_shape = jax.ShapeDtypeStruct((4,) + block, F32)
    raw = pltpu.VMEM((n.tiles + 1, planes * rows, LANES), F32)
    thin = pltpu.VMEM((n.tiles + 1, 2, thin_count, LANES), F32)
    weights = pltpu.VMEM((n.pairs, 6 * LANES), BF16)
    semaphores = pltpu.SemaphoreType.DMA
    by_own = pltpu.VMEM(t["by"].shape[1:], F32)
    bz_own = pltpu.VMEM(t["bz_e"].shape[1:], BF16)

    def params(mebibytes):
        return pltpu.CompilerParams(vmem_limit_bytes=mebibytes * 2**20)

    def cost(us):
        return pl.CostEstimate(flops=int(us * 1e9), bytes_accessed=int(us * 3e6), transcendentals=0)

    blocks = [pltpu.VMEM(block, F32)] * 3
    speeds = pltpu.VMEM((4,) + block, F32)
    speed, field, spare, image = pl.pallas_call(
        functools.partial(inner_kernel, n),
        in_specs=[small, held, held, outside, outside, held] + [outside] * 4,
        out_specs=[outside] * 4,
        out_shape=[speed_shape, field_shape, field_shape, field_shape],
        scratch_shapes=[
            speeds, *blocks, raw, raw, weights, by_own, bz_own,
            semaphores((2, n.tiles + 1)), semaphores((2,)), semaphores((2, 4)), semaphores((3,)),
        ],
        compiler_params=params(60),
        cost_estimate=cost(20),
    )(
        place, modes, t["bx"], t["by"], t["bz_e"], t["spread"], adjoint_field.reshape(flat), side_a,
        brain_image.reshape(flat), side_b,
    )

    sent_b = (rows_sent(brain_image[:, -HALO:]), rows_sent(brain_image[:, :HALO]))
    low_a, high_a, last_b, first_b, field = lax.optimization_barrier(
        (low_a, high_a, *sent_b, field)
    )
    corner_a = corners(low_a, high_a, thin_count)
    low_b, high_b = to_neighbours(last_b, first_b)

    kept, given, adjoint_end = pl.pallas_call(
        functools.partial(outer_kernel, n),
        in_specs=[small] + [outside] * 4 + [held] * 3 + [outside] * 6,
        out_specs=[held, held, outside],
        out_shape=[
            jax.ShapeDtypeStruct((3 * n.chunk // 2, LANES), F32),
            jax.ShapeDtypeStruct((3 * n.chunk // 2, LANES), F32),
            jax.ShapeDtypeStruct(flat, F32),
        ],
        scratch_shapes=[
            speeds,
            *blocks,
            raw,
            thin,
            pltpu.VMEM((n.tiles, 2, planes, LANES), F32),
            pltpu.VMEM((3, planes * rows, n.wide), BF16),
            pltpu.VMEM((3, planes * rows, n.wide), BF16),
            pltpu.VMEM((n.pairs, LANES), F32),
            pltpu.VMEM(t["by_t"].shape[1:], F32),
            pltpu.VMEM(t["bz_p"].shape[1:], BF16),
            semaphores((2 * n.tiles + 2,)),
            semaphores((2 * n.tiles,)),
            semaphores((n.tiles,)),
            semaphores((2,)),
            semaphores((2, 4)),
            semaphores((3,)),
            pltpu.VMEM((3 * n.chunk, LANES), F32),
        ],
        compiler_params=params(60),
        cost_estimate=cost(16),
    )(
        place, speed, field, spare, image, t["spread"], t["gather"], t["bx_t"], t["by_t"], t["bz_p"],
        low_a, high_a, *corner_a,
    )
    kept, given, low_b, high_b = lax.optimization_barrier((kept, given, low_b, high_b))
    kept, other = sum_over_devices(kept, given)
    corner_b = corners(low_b, high_b, thin_count)
    image_end, updated = pl.pallas_call(
        functools.partial(last_kernel, n),
        in_specs=[small] + [held] * 5 + [outside, outside, held, held] + [outside] * 5,
        out_specs=[outside, held],
        out_shape=[
            jax.ShapeDtypeStruct(flat, F32),
            jax.ShapeDtypeStruct((3, n.pairs, n.modes), F32),
        ],
        scratch_shapes=[
            speeds,
            *blocks[:2],
            raw,
            thin,
            weights,
            by_own,
            bz_own,
            semaphores((2 * n.tiles + 2,)),
            semaphores((n.tiles,)),
            semaphores((2,)),
            semaphores((1,)),
        ],
        compiler_params=params(60),
        cost_estimate=cost(28),
    )(
        place, modes, kept, other, t["factor"], t["bx"], t["by"], t["bz_e"], t["spread"], t["gather"],
        image, low_b, high_b, *corner_b,
    )
    return (
        adjoint_end.reshape(brain_image.shape),
        image_end.reshape(brain_image.shape),
        updated.reshape(velocity_modes.shape),
    )


def solution(mesh):
    placed = (P("subj", "ha", "dev"), P("subj", "ha", "dev"), P("subj", None, None, None))
    return jax.shard_map(
        per_device,
        mesh=mesh,
        in_specs=placed,
        out_specs=placed,
        check_vma=False,
    )
```
